32 devices in a mesh: groups: 1, mode: 32 (over z, y, x, core).
Axes of the slice: x: 2, y: 2, z: 4, core: 2. Of those that a mesh axis runs over, the one named last changes fastest.
Arguments:
- basis: bfloat16 [384, 16384], P('groups', 'mode')
- slab_region: int32 [128], P(('groups', 'mode')), may hold values from 0 to 8
- coef_index: int32 [9, 6], P('groups'), may hold values from 0 to 8
- coef_table: float32 [8], P('groups'), may hold values from 0.2 to 5
Outputs:
- gram: float32 [21, 384, 384], P(None, ('groups', 'mode'))
The draws below stay inside these ranges and needn't reach their ends.
All inputs are finite; a program needn't handle non-finite values.
Results may differ from the reference program's by a relative error of at most 0.0005.
The reference program's roundings to bfloat16 on the way (of `actions`) count: a program that leaves them out, or rounds other values in their place, can miss the bound.
Values may be sent and summed in bfloat16 or wider, within the bound.
No kernel may reach another device: no remote copies, remote signals or barrier semaphores. Data moves between devices by JAX's collectives and lax.ppermute only.
A program may use at most 128 MiB of HBM per device.

```python
import math
import jax
import jax.numpy as jnp
from jax import lax

NB = 384
SLABW = 128
REGIONS = 9
TERMS = 6
NCOEF = 8
SLABS = 128
CELLS = 16384
N_MODE = 32


def draw_basis(key, part):
    key_mode = jax.random.fold_in(jax.random.fold_in(key, 17), 0)
    key_cell = jax.random.fold_in(jax.random.fold_in(key, 17), 1)
    key_main = jax.random.fold_in(jax.random.fold_in(key, 17), 2)
    key_pair = jax.random.fold_in(jax.random.fold_in(key, 17), 4)
    mode_scale = jnp.exp(math.log(10.0) * jax.random.uniform(key_mode, (NB,), jnp.float32) - math.log(10.0) * 0.5)
    ramp = jnp.arange(CELLS, dtype=jnp.float32) / CELLS
    cell_scale = jnp.exp(math.log(3.0) * ramp + math.log(3.0) * jax.random.uniform(key_cell, (CELLS,), jnp.float32))
    cell_block = jnp.arange(CELLS, dtype=jnp.int32) // (CELLS // N_MODE)
    mode_block = jnp.arange(NB, dtype=jnp.int32) // (NB // N_MODE)
    pairing = jax.random.permutation(key_pair, N_MODE)
    boost = jnp.where(pairing[cell_block][None, :] == mode_block[:, None], 4.0, 1.0)
    values = jnp.clip(jax.random.normal(key_main, (NB, CELLS), jnp.float32), -6.0, 6.0)
    return (boost * mode_scale[:, None] * cell_scale[None, :] * values).astype(jnp.bfloat16)


def touch_ends(values, rng, least, largest):
    longest = values.shape.index(max(values.shape))
    spots = []
    for shift in (0, 1):
        where = [jax.random.randint(jax.random.fold_in(rng, axis), (), 0, length) for axis, length in enumerate(values.shape)]
        where[longest] = (where[longest] + shift) % values.shape[longest]
        spots.append(tuple(where))
    return values.at[spots[0]].set(least).at[spots[1]].set(largest)


def setup_inputs(seed: int = 0, part: int = 0) -> dict:
    arg_keys = jax.random.split(jax.random.key(seed), 5)
    own_keys = jax.random.split(jax.random.fold_in(arg_keys[4], part), 5)
    basis = draw_basis(jax.random.fold_in(jax.random.fold_in(arg_keys[4], part), 71), part)
    slab_region = touch_ends(jax.random.randint(own_keys[1], (SLABS,), 0, REGIONS), jax.random.fold_in(own_keys[1], 1), 0, REGIONS - 1).astype(jnp.int32)
    coef_index = touch_ends(jax.random.randint(own_keys[2], (REGIONS, TERMS), 0, NCOEF + 1), jax.random.fold_in(own_keys[2], 1), 0, NCOEF).astype(jnp.int32)
    coef_table = jnp.clip(jnp.exp(jax.random.uniform(own_keys[3], (NCOEF,), jnp.float32, math.log(0.2), math.log(5.0))), 0.2, 5.0)
    return {"basis": basis, "slab_region": slab_region, "coef_index": coef_index, "coef_table": coef_table}


def slab_weights(slab_region, coef_index, coef_table):
    table_hit = (coef_index[:, :, None] == jnp.arange(NCOEF, dtype=jnp.int32)[None, None, :]).astype(jnp.float32)
    kappa = lax.optimization_barrier(jnp.sum(table_hit * coef_table[None, None, :], axis=2))
    region_hit = (slab_region[:, None] == jnp.arange(REGIONS, dtype=jnp.int32)[None, :]).astype(jnp.float32)
    return lax.optimization_barrier(jnp.sum(region_hit[:, :, None] * kappa[None, :, :], axis=1))

def one_action(field, weight, term):
    rows = field.shape[0]
    if term == 0:
        stencil = 2.0 * field - jnp.roll(field, 1, axis=1) - jnp.roll(field, -1, axis=1)
    elif term == 1:
        zero_col = jnp.zeros((rows, SLABS, 1), jnp.float32)
        left_w = jnp.concatenate([zero_col, field[:, :, :-1]], axis=2)
        right_w = jnp.concatenate([field[:, :, 1:], zero_col], axis=2)
        stencil = 2.0 * field - left_w - right_w
    elif term == 2:
        stencil = field - jnp.roll(field, 1, axis=1)
    elif term == 3:
        stencil = field - jnp.roll(field, -1, axis=1)
    elif term == 4:
        stencil = field - field[:, :, ::-1]
    else:
        stencil = field
    return (weight[None, :, None] * stencil).reshape(rows, SLABS * SLABW).astype(jnp.bfloat16)

def reference(basis, slab_region, coef_index, coef_table):
    slab_kappa = slab_weights(slab_region, coef_index, coef_table)
    field = basis.astype(jnp.float32).reshape(NB, SLABS, SLABW)
    actions = [one_action(field, slab_kappa[:, term], term) for term in range(TERMS)]
    sums = []
    for term in range(TERMS):
        values = actions[term].astype(jnp.float32)
        sums.append(jnp.sum(values * values))
    level = jnp.stack(sums) / (NB * CELLS) + 1e-06
    blocks = []
    for first in range(TERMS):
        for second in range(first, TERMS):
            raw = jnp.dot(actions[first], actions[second].T, preferred_element_type=jnp.float32)
            blocks.append(raw / (CELLS * jnp.sqrt(level[first] * level[second])))
    return jnp.stack(blocks, axis=0)
```

```python
import functools

import jax
import jax.numpy as jnp
from jax import lax
from jax.experimental import pallas as pl
from jax.experimental.pallas import tpu as pltpu
from jax.sharding import PartitionSpec as P

GROUP = 8
KROWS = 32
LIMIT = 2.0**15
F32 = jnp.float32
BF16 = jnp.bfloat16
VMEM = pl.BlockSpec(memory_space=pltpu.VMEM)
SMEM = pl.BlockSpec(memory_space=pltpu.SMEM)


def params():
    return pltpu.CompilerParams(vmem_limit_bytes=40 * 1024 * 1024)


def shape(dims, dtype=F32):
    return jax.ShapeDtypeStruct(dims, dtype)


def payload_kernel(basis, region, index, table, first, second):
    rows, cells = basis.shape
    slabs = region.shape[0]
    width = cells // slabs
    terms = index.shape[1]
    entries = table.shape[0]
    half = first.shape[0]
    row = lax.broadcasted_iota(jnp.int32, (KROWS, width), 0)
    for s in range(slabs):
        reg = region[s]
        block = jnp.zeros((KROWS, width), F32)
        for q in range(terms):
            at = index[reg, q]
            kappa = jnp.where(at < entries, table[jnp.minimum(at, entries - 1)], 0.0)
            full = jnp.full((KROWS, width), kappa, F32)
            high = full.astype(BF16).astype(F32)
            mid = (full - high).astype(BF16).astype(F32)
            low = (full - high - mid).astype(BF16).astype(F32)
            block = jnp.where(row == 3 * q, high, block)
            block = jnp.where(row == 3 * q + 1, mid, block)
            block = jnp.where(row == 3 * q + 2, low, block)
        first[0:KROWS, s * width : (s + 1) * width] = block.astype(BF16)
    first[KROWS:half, :] = basis[0 : half - KROWS, :]
    second[...] = basis[half - KROWS :, :]


def payload(basis, region, index, table):
    rows, cells = basis.shape
    half = (rows + KROWS) // 2
    return pl.pallas_call(
        payload_kernel,
        out_shape=(shape((half, cells), BF16), shape((half, cells), BF16)),
        in_specs=[VMEM, SMEM, SMEM, SMEM],
        out_specs=(VMEM, VMEM),
        compiler_params=params(),
    )(basis, region, index, table)


def flip(values, mask, count):
    return lax.ppermute(values, "mode", [(i, i ^ mask) for i in range(count)])


def gather(first, second, count):
    x, y, core = 2, 4, 1
    fx, sy = flip(first, x, count), flip(second, y, count)
    fy, sx = flip(first, y, count), flip(second, x, count)
    fxy, sxy = flip(fx, y, count), flip(sy, x, count)
    firsts = {0: first, 2: fx, 4: fy, 6: fxy}
    seconds = {0: second, 2: sx, 4: sy, 6: sxy}
    for mask in (0, 2, 4, 6):
        firsts[mask + 1] = flip(firsts[mask], core, count)
        seconds[mask + 1] = flip(seconds[mask], core, count)
    return [firsts[m] for m in range(GROUP)] + [seconds[m] for m in range(GROUP)]


def place(count):
    me = lax.axis_index("mode")
    return lax.rem(me, GROUP), lax.div(me, GROUP)


def selector(own, rows, planes):
    j, a = place(None)
    line = lax.broadcasted_iota(jnp.int32, (planes * own, rows), 0)
    column = lax.broadcasted_iota(jnp.int32, (planes * own, rows), 1)
    shift = jnp.zeros((planes * own, rows), jnp.int32)
    for k in range(planes):
        start = lax.rem(a + k, planes) * (GROUP * own) + j * own - k * own
        shift = jnp.where(line >= k * own, start, shift)
    return jnp.where(column - line == shift, 1.0, 0.0).astype(BF16)


def assemble_kernel(own, planes, *refs):
    pieces, (field, weights) = refs[: 2 * GROUP], refs[2 * GROUP :]
    j, _ = place(None)
    half, cells = pieces[0].shape
    width = field.shape[2]
    slabs = cells // width
    rows = 2 * half - KROWS
    pick = selector(own, rows, planes)
    for mask in range(GROUP):
        owner = jnp.bitwise_xor(j, mask)
        for s in range(slabs):
            lanes = slice(s * width, (s + 1) * width)
            weights[owner * slabs + s] = pieces[mask][0:KROWS, lanes]
            block = jnp.concatenate(
                [pieces[mask][KROWS:half, lanes], pieces[GROUP + mask][:, lanes]], axis=0
            )
            field[owner * slabs + s, 0:rows] = block
            field[owner * slabs + s, rows:] = jnp.dot(
                pick, block, preferred_element_type=F32
            ).astype(BF16)


def assemble(pieces, own, planes, width):
    half, cells = pieces[0].shape
    slabs = GROUP * (cells // width)
    rows = 2 * half - KROWS
    return pl.pallas_call(
        functools.partial(assemble_kernel, own, planes),
        out_shape=(
            shape((slabs, rows + planes * own, width), BF16),
            shape((slabs, KROWS, width), BF16),
        ),
        in_specs=[VMEM] * (2 * GROUP),
        out_specs=(VMEM, VMEM),
        compiler_params=params(),
    )(*pieces)


def across(width):
    line = lax.broadcasted_iota(jnp.int32, (width, width), 0)
    column = lax.broadcasted_iota(jnp.int32, (width, width), 1)
    same = jnp.where(line == column, 1.0, 0.0)
    beside = jnp.where(jnp.abs(line - column) == 1, 1.0, 0.0)
    mirror = jnp.where(line + column == width - 1, 1.0, 0.0)
    return jnp.concatenate([2.0 * same - beside, same - mirror], axis=1).astype(BF16)


def act(triples, weights, stencil, side, right, left, squares, rows, terms):
    total = triples[0][1].shape[0]
    own = total - rows
    width = triples[0][1].shape[1]
    chunk = own
    for n, (before, here, after, weight) in enumerate(triples):
        lanes = slice(n * width, (n + 1) * width)
        side[...] = jnp.dot(here[...], stencil, preferred_element_type=F32)
        table = weight[...].astype(F32)
        kappas = []
        for q in range(terms):
            one = table[3 * q : 3 * q + 1] + table[3 * q + 1 : 3 * q + 2] + table[3 * q + 2 : 3 * q + 3]
            kappas.append(jnp.broadcast_to(one, (8, width))[None])
        sums = [jnp.zeros((8, width), F32) for _ in range(terms)]
        for start in range(0, total, chunk):
            part = slice(start, start + chunk)
            value = here[part, :].astype(F32)
            back = value - before[part, :].astype(F32)
            ahead = value - after[part, :].astype(F32)
            shapes = (
                back + ahead,
                side[part, 0:width],
                back,
                ahead,
                side[part, width : 2 * width],
                value,
            )
            for q in range(terms):
                action = (shapes[q].reshape(chunk // 8, 8, width) * kappas[q]).reshape(chunk, width)
                action = action.astype(BF16)
                if start < rows:
                    right[q, part, lanes] = action
                    back32 = action.astype(F32)
                    sums[q] += jnp.sum((back32 * back32).reshape(chunk // 8, 8, width), axis=0)
                else:
                    left[q * own : (q + 1) * own, lanes] = action
        for q in range(terms):
            squares[q] += sums[q]


def contract(left, right, total, own, terms):
    offset = 0
    for k in range(terms):
        lines = own * (k + 1)
        total[offset : offset + lines, :] += lax.dot_general(
            left[0:lines, :],
            right[k],
            (((1,), (1,)), ((), ())),
            preferred_element_type=F32,
        )
        offset += lines


def inner_kernel(rows, terms, field, weights, total, squares, side, right, left):
    slabs = field.shape[0]
    own = field.shape[1] - rows
    stencil = across(field.shape[2])
    total[...] = jnp.zeros_like(total)
    squares[...] = jnp.zeros_like(squares)

    @pl.loop(0, (slabs - 2) // 2)
    def _(t):
        s = 2 * t + 1
        triples = [
            (field.at[s + n - 1], field.at[s + n], field.at[s + n + 1], weights.at[s + n])
            for n in range(2)
        ]
        act(triples, weights, stencil, side, right, left, squares, rows, terms)
        contract(left, right, total, own, terms)


def outer_kernel(
    rows, terms, own, planes, field, weights, low, high, total_in, squares_in,
    mine, others, levels, total, squares, ends, side, right, left,
):
    slabs, every, width = field.shape
    lines = every - rows
    stencil = across(width)
    pick = selector(own, rows, planes)
    total[...] = total_in[...]
    squares[...] = squares_in[...]
    for n, halo in enumerate((low, high)):
        ends[n, 0:rows] = halo[...]
        ends[n, rows:] = jnp.dot(pick, halo[...], preferred_element_type=F32).astype(BF16)
    triples = [
        (ends.at[0], field.at[0], field.at[1], weights.at[0]),
        (field.at[slabs - 2], field.at[slabs - 1], ends.at[1], weights.at[slabs - 1]),
    ]
    act(triples, weights, stencil, side, right, left, squares, rows, terms)
    contract(left, right, total, lines, terms)
    norms = []
    for q in range(terms):
        level = jnp.sum(squares[q], keepdims=True)
        levels[q] = jnp.broadcast_to(level, levels.shape[1:])
        norms.append(LIMIT**0.5 * lax.rsqrt(jnp.maximum(level, 1e-30)))
    offset = 0
    for k in range(terms):
        for q in range(k + 1):
            scale = norms[q] * norms[k]
            pair = q * terms - q * (q - 1) // 2 + k - q
            for z in range(planes):
                at = offset + q * lines + z * own
                part = total[at : at + own, :] * scale
                if z == 0:
                    mine[pair * own : (pair + 1) * own, :] = part
                else:
                    others[z - 1, pair * own : (pair + 1) * own, :] = part
        offset += (k + 1) * lines


def products(field, weights, count, rows, own, planes, terms):
    slabs, every, width = field.shape
    lines = every - rows
    pairs = terms * (terms + 1) // 2
    scratch = [
        pltpu.VMEM((every, 2 * width), F32),
        pltpu.VMEM((terms, rows, 2 * width), BF16),
        pltpu.VMEM((terms * lines, 2 * width), BF16),
    ]
    ahead = [(i, (i + GROUP) % count) for i in range(count)]
    behind = [(i, (i - GROUP) % count) for i in range(count)]
    low = lax.ppermute(field[slabs - 1, :rows], "mode", ahead)
    high = lax.ppermute(field[0, :rows], "mode", behind)
    total, squares = pl.pallas_call(
        functools.partial(inner_kernel, rows, terms),
        out_shape=(shape((pairs * lines, rows)), shape((terms, 8, width))),
        in_specs=[VMEM, VMEM],
        out_specs=(VMEM, VMEM),
        scratch_shapes=scratch,
        compiler_params=params(),
        cost_estimate=pl.CostEstimate(flops=20_000_000_000, bytes_accessed=5_000_000, transcendentals=0),
    )(field, weights)
    return pl.pallas_call(
        functools.partial(outer_kernel, rows, terms, own, planes),
        out_shape=(
            shape((pairs * own, rows)),
            shape((planes - 1, pairs * own, rows)),
            shape((terms, 8, width)),
        ),
        in_specs=[VMEM] * 6,
        out_specs=(VMEM, VMEM, VMEM),
        scratch_shapes=[
            pltpu.VMEM((pairs * lines, rows), F32),
            pltpu.VMEM((terms, 8, width), F32),
            pltpu.VMEM((2, every, width), BF16),
            *scratch,
        ],
        compiler_params=params(),
    )(field, weights, low, high, total, squares)


def per_device(basis, slab_region, coef_index, coef_table):
    terms = coef_index.shape[1]
    rows, cells = basis.shape
    width = cells // slab_region.shape[0]
    count = lax.axis_size("mode")
    planes = count // GROUP
    own = rows // count
    pairs = [(q, k) for q in range(terms) for k in range(q, terms)]
    first, second = payload(basis, slab_region, coef_index, coef_table)
    pieces = gather(first, second, count)
    field, weights = assemble(pieces, own, planes, width)
    mine, others, levels = products(field, weights, count, rows, own, planes, terms)
    sums = [levels[:, 0, 0]]
    parts = [mine]
    others = others.astype(jnp.float16)
    for z in range(1, planes):
        there = [(i, (i + z * GROUP) % count) for i in range(count)]
        sums.append(lax.ppermute(levels, "mode", there)[:, 0, 0])
        parts.append(lax.ppermute(others[z - 1], "mode", there).astype(F32))
    level = sum(sums) / (rows * cells * count) + 1e-06
    root = lax.rsqrt(level)
    out = 0.0
    for part, one in zip(parts, sums):
        decode = jnp.sqrt(jnp.maximum(one, 1e-30)) * root
        factor = jnp.stack([decode[q] * decode[k] for q, k in pairs]) / (LIMIT * cells * count)
        out = out + part.reshape(len(pairs), own, rows) * factor[:, None, None]
    return out


def solution(mesh):
    return jax.shard_map(
        per_device,
        mesh=mesh,
        in_specs=(P("groups", "mode"), P(("groups", "mode")), P("groups", None), P("groups")),
        out_specs=P(None, ("groups", "mode"), None),
        check_vma=False,
    )
```

```python
import functools

import jax
import jax.numpy as jnp
from jax import lax
from jax.experimental import pallas as pl
from jax.experimental.pallas import tpu as pltpu
from jax.sharding import PartitionSpec as P

GROUP = 8
KROWS = 32
LIMIT = 2.0**15
F32 = jnp.float32
BF16 = jnp.bfloat16
VMEM = pl.BlockSpec(memory_space=pltpu.VMEM)
SMEM = pl.BlockSpec(memory_space=pltpu.SMEM)


def params():
    return pltpu.CompilerParams(vmem_limit_bytes=40 * 1024 * 1024)


def shape(dims, dtype=F32):
    return jax.ShapeDtypeStruct(dims, dtype)


def payload_kernel(basis, region, index, table, first, second):
    rows, cells = basis.shape
    slabs = region.shape[0]
    width = cells // slabs
    terms = index.shape[1]
    entries = table.shape[0]
    half = first.shape[0]
    row = lax.broadcasted_iota(jnp.int32, (KROWS, width), 0)
    for s in range(slabs):
        reg = region[s]
        block = jnp.zeros((KROWS, width), F32)
        for q in range(terms):
            at = index[reg, q]
            kappa = jnp.where(at < entries, table[jnp.minimum(at, entries - 1)], 0.0)
            full = jnp.full((KROWS, width), kappa, F32)
            high = full.astype(BF16).astype(F32)
            mid = (full - high).astype(BF16).astype(F32)
            low = (full - high - mid).astype(BF16).astype(F32)
            block = jnp.where(row == 3 * q, high, block)
            block = jnp.where(row == 3 * q + 1, mid, block)
            block = jnp.where(row == 3 * q + 2, low, block)
        first[0:KROWS, s * width : (s + 1) * width] = block.astype(BF16)
    first[KROWS:half, :] = basis[0 : half - KROWS, :]
    second[...] = basis[half - KROWS :, :]


def payload(basis, region, index, table):
    rows, cells = basis.shape
    half = (rows + KROWS) // 2
    return pl.pallas_call(
        payload_kernel,
        out_shape=(shape((half, cells), BF16), shape((half, cells), BF16)),
        in_specs=[VMEM, SMEM, SMEM, SMEM],
        out_specs=(VMEM, VMEM),
        compiler_params=params(),
    )(basis, region, index, table)


def flip(values, mask, count):
    return lax.ppermute(values, "mode", [(i, i ^ mask) for i in range(count)])


def gather(first, second, count):
    x, y, core = 2, 4, 1
    fx, sy = flip(first, x, count), flip(second, y, count)
    fy, sx = flip(first, y, count), flip(second, x, count)
    fxy, sxy = flip(fx, y, count), flip(sy, x, count)
    firsts = {0: first, 2: fx, 4: fy, 6: fxy}
    seconds = {0: second, 2: sx, 4: sy, 6: sxy}
    for mask in (0, 2, 4, 6):
        firsts[mask + 1] = flip(firsts[mask], core, count)
        seconds[mask + 1] = flip(seconds[mask], core, count)
    return [firsts[m] for m in range(GROUP)] + [seconds[m] for m in range(GROUP)]


def place(count):
    me = lax.axis_index("mode")
    return lax.rem(me, GROUP), lax.div(me, GROUP)


def selector(own, rows, planes):
    j, a = place(None)
    line = lax.broadcasted_iota(jnp.int32, (planes * own, rows), 0)
    column = lax.broadcasted_iota(jnp.int32, (planes * own, rows), 1)
    shift = jnp.zeros((planes * own, rows), jnp.int32)
    for k in range(planes):
        start = lax.rem(a + k, planes) * (GROUP * own) + j * own - k * own
        shift = jnp.where(line >= k * own, start, shift)
    return jnp.where(column - line == shift, 1.0, 0.0).astype(BF16)


def assemble_kernel(own, planes, *refs):
    pieces, (field, weights) = refs[: 2 * GROUP], refs[2 * GROUP :]
    j, _ = place(None)
    half, cells = pieces[0].shape
    width = field.shape[2]
    slabs = cells // width
    rows = 2 * half - KROWS
    pick = selector(own, rows, planes)
    for mask in range(GROUP):
        owner = jnp.bitwise_xor(j, mask)
        for s in range(slabs):
            lanes = slice(s * width, (s + 1) * width)
            weights[owner * slabs + s] = pieces[mask][0:KROWS, lanes]
            block = jnp.concatenate(
                [pieces[mask][KROWS:half, lanes], pieces[GROUP + mask][:, lanes]], axis=0
            )
            field[owner * slabs + s, 0:rows] = block
            field[owner * slabs + s, rows:] = jnp.dot(
                pick, block, preferred_element_type=F32
            ).astype(BF16)


def assemble(pieces, own, planes, width):
    half, cells = pieces[0].shape
    slabs = GROUP * (cells // width)
    rows = 2 * half - KROWS
    return pl.pallas_call(
        functools.partial(assemble_kernel, own, planes),
        out_shape=(
            shape((slabs, rows + planes * own, width), BF16),
            shape((slabs, KROWS, width), BF16),
        ),
        in_specs=[VMEM] * (2 * GROUP),
        out_specs=(VMEM, VMEM),
        compiler_params=params(),
    )(*pieces)


def across(width):
    line = lax.broadcasted_iota(jnp.int32, (width, width), 0)
    column = lax.broadcasted_iota(jnp.int32, (width, width), 1)
    same = jnp.where(line == column, 1.0, 0.0)
    beside = jnp.where(jnp.abs(line - column) == 1, 1.0, 0.0)
    mirror = jnp.where(line + column == width - 1, 1.0, 0.0)
    return jnp.concatenate([2.0 * same - beside, same - mirror], axis=1).astype(BF16)


def act(triples, weights, stencil, side, right, left, squares, rows, terms):
    total = triples[0][1].shape[0]
    own = total - rows
    width = triples[0][1].shape[1]
    chunk = own
    for n, (before, here, after, weight) in enumerate(triples):
        lanes = slice(n * width, (n + 1) * width)
        side[...] = jnp.dot(here[...], stencil, preferred_element_type=F32)
        table = weight[...].astype(F32)
        kappas = []
        for q in range(terms):
            one = table[3 * q : 3 * q + 1] + table[3 * q + 1 : 3 * q + 2] + table[3 * q + 2 : 3 * q + 3]
            kappas.append(jnp.broadcast_to(one, (8, width))[None])
        sums = [jnp.zeros((8, width), F32) for _ in range(terms)]
        for start in range(0, total, chunk):
            part = slice(start, start + chunk)
            value = here[part, :].astype(F32)
            back = value - before[part, :].astype(F32)
            ahead = value - after[part, :].astype(F32)
            shapes = (
                back + ahead,
                side[part, 0:width],
                back,
                ahead,
                side[part, width : 2 * width],
                value,
            )
            for q in range(terms):
                action = (shapes[q].reshape(chunk // 8, 8, width) * kappas[q]).reshape(chunk, width)
                action = action.astype(BF16)
                if start < rows:
                    right[q, part, lanes] = action
                    back32 = action.astype(F32)
                    sums[q] += jnp.sum((back32 * back32).reshape(chunk // 8, 8, width), axis=0)
                else:
                    left[q * own : (q + 1) * own, lanes] = action
        for q in range(terms):
            squares[q] += sums[q]


def contract(left, right, total, own, terms):
    offset = 0
    for k in range(terms):
        lines = own * (k + 1)
        total[offset : offset + lines, :] += lax.dot_general(
            left[0:lines, :],
            right[k],
            (((1,), (1,)), ((), ())),
            preferred_element_type=F32,
        )
        offset += lines


def inner_kernel(rows, terms, field, weights, total, squares, side, right, left):
    slabs = field.shape[0]
    own = field.shape[1] - rows
    stencil = across(field.shape[2])
    total[...] = jnp.zeros_like(total)
    squares[...] = jnp.zeros_like(squares)

    @pl.loop(0, (slabs - 2) // 2)
    def _(t):
        s = 2 * t + 1
        triples = [
            (field.at[s + n - 1], field.at[s + n], field.at[s + n + 1], weights.at[s + n])
            for n in range(2)
        ]
        act(triples, weights, stencil, side, right, left, squares, rows, terms)
        contract(left, right, total, own, terms)


def outer_kernel(
    rows, terms, own, planes, field, weights, low, high, total_in, squares_in,
    mine, others, levels, total, squares, ends, side, right, left,
):
    slabs, every, width = field.shape
    lines = every - rows
    stencil = across(width)
    pick = selector(own, rows, planes)
    total[...] = total_in[...]
    squares[...] = squares_in[...]
    for n, halo in enumerate((low, high)):
        ends[n, 0:rows] = halo[...]
        ends[n, rows:] = jnp.dot(pick, halo[...], preferred_element_type=F32).astype(BF16)
    triples = [
        (ends.at[0], field.at[0], field.at[1], weights.at[0]),
        (field.at[slabs - 2], field.at[slabs - 1], ends.at[1], weights.at[slabs - 1]),
    ]
    act(triples, weights, stencil, side, right, left, squares, rows, terms)
    contract(left, right, total, lines, terms)
    norms = []
    for q in range(terms):
        level = jnp.sum(squares[q], keepdims=True)
        levels[q] = jnp.broadcast_to(level, levels.shape[1:])
        norms.append(LIMIT**0.5 * lax.rsqrt(jnp.maximum(level, 1e-30)))
    offset = 0
    for k in range(terms):
        for q in range(k + 1):
            scale = norms[q] * norms[k]
            pair = q * terms - q * (q - 1) // 2 + k - q
            for z in range(planes):
                at = offset + q * lines + z * own
                part = total[at : at + own, :] * scale
                if z == 0:
                    mine[pair * own : (pair + 1) * own, :] = part
                else:
                    others[z - 1, pair * own : (pair + 1) * own, :] = part
        offset += (k + 1) * lines


def products(field, weights, count, rows, own, planes, terms):
    slabs, every, width = field.shape
    lines = every - rows
    pairs = terms * (terms + 1) // 2
    scratch = [
        pltpu.VMEM((every, 2 * width), F32),
        pltpu.VMEM((terms, rows, 2 * width), BF16),
        pltpu.VMEM((terms * lines, 2 * width), BF16),
    ]
    ahead = [(i, (i + GROUP) % count) for i in range(count)]
    behind = [(i, (i - GROUP) % count) for i in range(count)]
    low = lax.ppermute(field[slabs - 1, :rows], "mode", ahead)
    high = lax.ppermute(field[0, :rows], "mode", behind)
    total, squares = pl.pallas_call(
        functools.partial(inner_kernel, rows, terms),
        out_shape=(shape((pairs * lines, rows)), shape((terms, 8, width))),
        in_specs=[VMEM, VMEM],
        out_specs=(VMEM, VMEM),
        scratch_shapes=scratch,
        compiler_params=params(),
        cost_estimate=pl.CostEstimate(flops=20_000_000_000, bytes_accessed=5_000_000, transcendentals=0),
    )(field, weights)
    return pl.pallas_call(
        functools.partial(outer_kernel, rows, terms, own, planes),
        out_shape=(
            shape((pairs * own, rows)),
            shape((planes - 1, pairs * own, rows)),
            shape((terms, 8, width)),
        ),
        in_specs=[VMEM] * 6,
        out_specs=(VMEM, VMEM, VMEM),
        scratch_shapes=[
            pltpu.VMEM((pairs * lines, rows), F32),
            pltpu.VMEM((terms, 8, width), F32),
            pltpu.VMEM((2, every, width), BF16),
            *scratch,
        ],
        compiler_params=params(),
    )(field, weights, low, high, total, squares)


def finish_kernel(own, terms, cells, *refs):
    planes = (len(refs) - 1) // 2
    parts, levels, out = refs[:planes], refs[planes : 2 * planes], refs[-1]
    rows = parts[0].shape[1]
    decodes = []
    for q in range(terms):
        sums = [level[q, 0:1, 0:1] for level in levels]
        root = lax.rsqrt(sum(sums) / (rows * cells) + 1e-06) * (LIMIT * cells) ** -0.5
        decodes.append([jnp.sqrt(jnp.maximum(one, 1e-30)) * root for one in sums])
    pair = 0
    for q in range(terms):
        for k in range(q, terms):
            here = slice(pair * own, (pair + 1) * own)
            total = 0.0
            for z in range(planes):
                total = total + parts[z][here, :] * (decodes[q][z] * decodes[k][z])
            out[:, pair, :] = total
            pair += 1


def per_device(basis, slab_region, coef_index, coef_table):
    terms = coef_index.shape[1]
    rows, cells = basis.shape
    width = cells // slab_region.shape[0]
    count = lax.axis_size("mode")
    planes = count // GROUP
    own = rows // count
    first, second = payload(basis, slab_region, coef_index, coef_table)
    pieces = gather(first, second, count)
    field, weights = assemble(pieces, own, planes, width)
    mine, others, levels = products(field, weights, count, rows, own, planes, terms)
    sums = [levels]
    parts = [mine]
    others = others.astype(jnp.float16)
    for z in range(1, planes):
        there = [(i, (i + z * GROUP) % count) for i in range(count)]
        sums.append(lax.ppermute(levels, "mode", there))
        parts.append(lax.ppermute(others[z - 1], "mode", there).astype(F32))
    out = pl.pallas_call(
        functools.partial(finish_kernel, own, terms, cells * count),
        out_shape=shape((own, terms * (terms + 1) // 2, rows)),
        in_specs=[VMEM] * (2 * planes),
        out_specs=VMEM,
        compiler_params=params(),
    )(*parts, *sums)
    return jnp.transpose(out, (1, 0, 2))


def solution(mesh):
    return jax.shard_map(
        per_device,
        mesh=mesh,
        in_specs=(P("groups", "mode"), P(("groups", "mode")), P("groups", None), P("groups")),
        out_specs=P(None, ("groups", "mode"), None),
        check_vma=False,
    )
```

```python
import functools

import jax
import jax.numpy as jnp
from jax import lax
from jax.experimental import pallas as pl
from jax.experimental.pallas import tpu as pltpu
from jax.sharding import PartitionSpec as P

GROUP = 8
CORE, X, Y = 1, 2, 4
KROWS = 32
TOP = 14.0
PAIR_LANES = 32
F32 = jnp.float32
BF16 = jnp.bfloat16
VMEM = pl.BlockSpec(memory_space=pltpu.VMEM)
HBM = pl.BlockSpec(memory_space=pltpu.HBM)


def call(kernel, outs, scratch=(), aliases=None, ins=None, flops=0):
    def run(*args):
        return pl.pallas_call(
            kernel,
            out_shape=outs,
            in_specs=[VMEM] * len(args) if ins is None else ins,
            out_specs=jax.tree.map(lambda _: VMEM, outs),
            scratch_shapes=list(scratch),
            input_output_aliases=aliases or {},
            compiler_params=pltpu.CompilerParams(vmem_limit_bytes=32 * 1024 * 1024),
            cost_estimate=pl.CostEstimate(
                flops=flops, bytes_accessed=1_000_000, transcendentals=0
            ),
        )(*args)

    return run


def shape(dims, dtype=F32):
    return jax.ShapeDtypeStruct(dims, dtype)


def place():
    me = lax.axis_index("mode")
    return lax.rem(me, GROUP), lax.div(me, GROUP)


def flip(values, mask, count):
    return lax.ppermute(values, "mode", [(i, i ^ mask) for i in range(count)])


def payload_kernel(basis, region, index, table, out, region_s, index_s, table_s, sems):
    copies = [
        pltpu.make_async_copy(basis, out.at[KROWS:], sems.at[0]),
        pltpu.make_async_copy(region, region_s, sems.at[1]),
        pltpu.make_async_copy(index, index_s, sems.at[2]),
        pltpu.make_async_copy(table, table_s, sems.at[3]),
    ]
    for copy in copies:
        copy.start()
    for copy in copies[1:]:
        copy.wait()
    slabs = region.shape[0]
    width = out.shape[1] // slabs
    terms = index.shape[0]
    entries = table.shape[0]
    row = lax.broadcasted_iota(jnp.int32, (KROWS, width), 0)
    for s in range(slabs):
        reg = region_s[s]
        block = jnp.zeros((KROWS, width), F32)
        for q in range(terms):
            at = index_s[q, reg]
            kappa = jnp.where(at < entries, table_s[jnp.minimum(at, entries - 1)], 0.0)
            block = jnp.where(lax.div(row, 3) == q, kappa, block)
        high = block.astype(BF16).astype(F32)
        mid = (block - high).astype(BF16).astype(F32)
        low = block - high - mid
        part = lax.rem(row, 3)
        block = jnp.where(part == 0, high, jnp.where(part == 1, mid, low))
        out[0:KROWS, s * width : (s + 1) * width] = block.astype(BF16)
    copies[0].wait()


def payload(basis, region, index, table):
    rows, cells = basis.shape
    return call(
        payload_kernel,
        shape((rows + KROWS, cells), BF16),
        [
            pltpu.SMEM(region.shape, jnp.int32),
            pltpu.SMEM(index.shape[::-1], jnp.int32),
            pltpu.SMEM(table.shape, F32),
            pltpu.SemaphoreType.DMA((4,)),
        ],
        ins=[HBM] * 4,
    )(basis, region, index.T, table)


def selector(own, rows, planes):
    j, a = place()
    line = lax.broadcasted_iota(jnp.int32, (planes * own, rows), 0)
    column = lax.broadcasted_iota(jnp.int32, (planes * own, rows), 1)
    shift = jnp.zeros((planes * own, rows), jnp.int32)
    for k in range(planes):
        start = lax.rem(a + k, planes) * (GROUP * own) + j * own - k * own
        shift = jnp.where(line >= k * own, start, shift)
    return jnp.where(column - line == shift, 1.0, 0.0).astype(BF16)


def across(width):
    line = lax.broadcasted_iota(jnp.int32, (width, width), 0)
    column = lax.broadcasted_iota(jnp.int32, (width, width), 1)
    same = jnp.where(line == column, 1.0, 0.0)
    beside = jnp.where(jnp.abs(line - column) == 1, 1.0, 0.0)
    mirror = jnp.where(line + column == width - 1, 1.0, 0.0)
    return jnp.concatenate([2.0 * same - beside, same - mirror], axis=1).astype(BF16)


def act(triples, stencil, side, right, left, squares, base, rows, terms):
    total, width = triples[0][1].shape
    own = total - rows
    for n, (before, here, after, weight) in enumerate(triples):
        lanes = pl.ds(base + n * width, width)
        side[...] = jnp.dot(here[...], stencil, preferred_element_type=F32)
        table = weight[...].astype(F32)
        kappas = []
        for q in range(terms):
            one = (table[3 * q : 3 * q + 1] + table[3 * q + 1 : 3 * q + 2]) + table[
                3 * q + 2 : 3 * q + 3
            ]
            kappas.append(jnp.broadcast_to(one, (8, width))[None])
        sums = [jnp.zeros((8, width), F32) for _ in range(terms)]
        for start in range(0, total, own):
            part = slice(start, start + own)
            value = here[part, :].astype(F32)
            back = value - before[part, :].astype(F32)
            ahead = value - after[part, :].astype(F32)
            shapes = (
                back + ahead,
                side[part, 0:width],
                back,
                ahead,
                side[part, width : 2 * width],
                value,
            )
            for q in range(terms):
                action = shapes[q].reshape(own // 8, 8, width) * kappas[q]
                action = action.reshape(own, width).astype(BF16)
                if start < rows:
                    right[q, part, lanes] = action
                    rounded = action.astype(F32).reshape(own // 8, 8, width)
                    sums[q] += jnp.sum(rounded * rounded, axis=0)
                else:
                    left[q * own : (q + 1) * own, lanes] = action
        for q in range(terms):
            squares[q] += sums[q]


def contract(left, right, total, own, terms, depth, first=False):
    offset = 0
    for k in range(terms):
        lines = own * (k + 1)
        product = lax.dot_general(
            left[0:lines, 0:depth],
            right[k, :, 0:depth],
            (((1,), (1,)), ((), ())),
            preferred_element_type=F32,
        )
        if first:
            total[offset : offset + lines, :] = product
        else:
            total[offset : offset + lines, :] += product
        offset += lines


def spread(pieces, pick, field, weights, rows):
    j, _ = place()
    width = field.shape[2]
    for flipped, piece in enumerate(pieces):
        core = jnp.bitwise_xor(jnp.bitwise_and(j, 1), flipped)
        slabs = piece[0].shape[1] // width
        for s in range(slabs):
            lanes = slice(s * width, (s + 1) * width)
            at = core * slabs + s
            weights[at] = piece[0][0:KROWS, lanes]
            start = KROWS
            done = 0
            for part in piece:
                size = part.shape[0] - start
                field[at, done : done + size] = part[start:, lanes]
                done += size
                start = 0
            field[at, rows:] = jnp.dot(
                pick, field[at, 0:rows], preferred_element_type=F32
            ).astype(BF16)


def inner(field, weights, stencil, side, right, left, squares, base, rows, terms):
    slabs, _, width = field.shape

    @pl.loop(0, (slabs - 2) // 2)
    def _(t):
        s = 2 * t + 1
        triples = [
            (field.at[s + n - 1], field.at[s + n], field.at[s + n + 1], weights.at[s + n])
            for n in range(2)
        ]
        start = pl.multiple_of(base + 2 * t * width, width)
        act(triples, stencil, side, right, left, squares, start, rows, terms)


def pick_into(ends, at, field, slot, taken):
    @pl.when(taken)
    def _():
        ends[at] = field[slot]


def seam(ours, theirs, ends, seam_weights, field_weights, mine_first):
    slabs = ours.shape[0]
    for taken, (one, two) in (
        (mine_first, (0, 1)),
        (jnp.logical_not(mine_first), (1, 0)),
    ):

        @pl.when(taken)
        def _():
            fields = (ours, theirs)
            ends[0] = fields[one][slabs - 2]
            ends[1] = fields[one][slabs - 1]
            ends[2] = fields[two][0]
            ends[3] = fields[two][1]
            seam_weights[0] = field_weights[one][slabs - 1]
            seam_weights[1] = field_weights[two][0]


def own_kernel(rows, terms, own, planes, *refs):
    mine, other, field, weights, total, squares, side, right, left = refs
    squares[...] = jnp.zeros_like(squares)
    spread([[mine], [other]], selector(own, rows, planes), field, weights, rows)
    inner(field, weights, across(field.shape[2]), side, right, left, squares, 0, rows, terms)
    depth = (field.shape[0] - 2) * field.shape[2]
    contract(left, right, total, planes * own, terms, depth, first=True)


def middle_kernel(rows, terms, own, planes, *refs):
    (by_x, by_y, others, own_field, own_weights, total_in, squares_in,
     field_x, weights_x, field_y, weights_y, total, squares,
     side, right, left, ends, end_weights) = refs
    j, _ = place()
    width = field_x.shape[2]
    stencil = across(width)
    pick = selector(own, rows, planes)
    height = by_x.shape[0]
    squares[...] = squares_in[...]
    spread([[by_x], [others.at[:height]]], pick, field_x, weights_x, rows)
    spread([[by_y], [others.at[height:]]], pick, field_y, weights_y, rows)
    depth = (field_x.shape[0] - 2) * width
    inner(field_x, weights_x, stencil, side, right, left, squares, 0, rows, terms)
    inner(field_y, weights_y, stencil, side, right, left, squares, depth, rows, terms)
    first = jnp.bitwise_and(j, X) == 0
    seam(own_field, field_x, ends, end_weights, (own_weights, weights_x), first)
    triples = [(ends.at[n], ends.at[n + 1], ends.at[n + 2], end_weights.at[n]) for n in range(2)]
    act(triples, stencil, side, right, left, squares, 2 * depth, rows, terms)
    total[...] = total_in[...]
    contract(left, right, total, planes * own, terms, 2 * depth + 2 * width)


def edge_kernel(*refs):
    pieces, strip = refs[:-1], refs[-1]
    j, _ = place()
    lines, cells = strip.shape
    parts = (pieces[0].shape[0] - KROWS) // lines
    width = cells // parts
    for piece, flips in zip(pieces, (0, CORE, X, Y)):
        for here, lanes in ((0, slice(0, width)), (GROUP - 1, slice(cells - width, cells))):

            @pl.when(jnp.bitwise_xor(j, flips) == here)
            def _():
                for n in range(parts):
                    strip[:, n * width : (n + 1) * width] = piece[
                        KROWS + n * lines : KROWS + (n + 1) * lines, lanes
                    ]


def last_kernel(rows, terms, own, planes, *refs):
    (one, two, strip, others_in, *rest) = refs
    fields, field_weights, rest = list(rest[:3]), list(rest[3:6]), rest[6:]
    (total_in, squares_in, mine, others, levels,
     field, weights, total, squares, side, right, left, ends, end_weights) = rest
    fields.append(field)
    field_weights.append(weights)
    slabs, every, width = field.shape
    lines = every - rows
    j, _ = place()
    chip = lax.div(j, 2)
    stencil = across(width)
    pick = selector(own, rows, planes)
    squares[...] = squares_in[...]
    height = one.shape[0] + two.shape[0]
    even = jnp.bitwise_and(j, CORE) == 0
    size = strip.shape[0]
    other = others_in[height:, :]
    first_core = jnp.where(even, strip[...], other)
    second_core = jnp.where(even, other, strip[...])
    for at, source in ((0, second_core), (5, first_core)):
        for n in range(rows // size):
            ends[at, n * size : (n + 1) * size] = source[:, n * width : (n + 1) * width]
        ends[at, rows:] = jnp.dot(pick, ends[at, 0:rows], preferred_element_type=F32).astype(BF16)
    spread([[one, two], [others_in.at[0:height]]], pick, field, weights, rows)
    inner(field, weights, stencil, side, right, left, squares, 0, rows, terms)
    for n, source in enumerate(fields):
        for number, at, slots, weight in (
            (0, 1, (0, 1), 0),
            (3, 3, (slabs - 2, slabs - 1), 1),
            (1, 6, (slabs - 2, slabs - 1), 2),
            (2, 8, (0, 1), 3),
        ):

            @pl.when(jnp.bitwise_xor(chip, n) == number)
            def _():
                ends[at] = source[slots[0]]
                ends[at + 1] = source[slots[1]]
                end_weights[weight] = field_weights[n][slots[1] if slots[0] else 0]

    first = jnp.bitwise_and(j, X) == 0
    seam(fields[2], field, ends.at[10:14], end_weights.at[4:6], (field_weights[2], weights), first)
    triples = [
        (ends.at[n - 1], ends.at[n], ends.at[n + 1], end_weights.at[m])
        for m, n in enumerate((1, 4, 7, 8, 11, 12))
    ]
    depth = (slabs - 2) * width
    for n in range(0, 6, 2):
        act(triples[n : n + 2], stencil, side, right, left, squares, depth + n * width, rows, terms)
    total[...] = total_in[...]
    contract(left, right, total, lines, terms, depth + 6 * width)
    lane = lax.broadcasted_iota(jnp.int32, (8, rows), 1)
    line = lax.broadcasted_iota(jnp.int32, (8, rows), 0)
    spare = jnp.zeros((8, rows), F32)
    for q in range(terms):
        level = jnp.sum(squares[q], keepdims=True)
        levels[q : q + 1, :] = jnp.broadcast_to(level, (1, levels.shape[1]))
        power = jnp.ceil(jnp.log2(jnp.maximum(level, 1e-30)))
        level = level * jnp.exp2(-power)
        high = jnp.floor(level * 2.0**10) * 2.0**-10
        low = (level - high) * 2.0**10
        low = jnp.floor(low * 2.0**10) * 2.0**-10
        for n, value in enumerate((power, high, low)):
            here = jnp.logical_and(line == 0, lane == PAIR_LANES + 3 * q + n)
            spare = jnp.where(here, value, spare)
    levels[terms:, :] = jnp.zeros((levels.shape[0] - terms, levels.shape[1]), F32)
    offset = 0
    for k in range(terms):
        for q in range(k + 1):
            pair = q * terms - q * (q - 1) // 2 + k - q
            at = offset + q * lines
            block = total[at : at + lines, :]
            largest = jnp.max(jnp.abs(block), keepdims=True)
            power = jnp.ceil(jnp.log2(jnp.maximum(largest, 1e-30)))
            spare = jnp.where(jnp.logical_and(line == 0, lane == pair), power, spare)
            scale = jnp.exp2(TOP - power)
            for z in range(planes):
                part = total[at + z * own : at + (z + 1) * own, :]
                if z == 0:
                    mine[pair * own : (pair + 1) * own, :] = part
                else:
                    others[z - 1, pair * own : (pair + 1) * own, :] = part * scale
        offset += (k + 1) * lines
    end = terms * (terms + 1) // 2 * own
    for z in range(1, planes):
        others[z - 1, end:, :] = spare[0 : others.shape[1] - end]


def finish_kernel(own, terms, cells, *refs):
    parts, (levels, out) = refs[:-2], refs[-2:]
    rows = parts[0].shape[1]
    pairs = terms * (terms + 1) // 2
    spares = [part[pairs * own : pairs * own + 1, 0:128] for part in parts[1:]]
    norms = []
    for q in range(terms):
        level = levels[q : q + 1, 0:1]
        for spare in spares:
            power, high, low = (
                spare[:, PAIR_LANES + 3 * q + n : PAIR_LANES + 3 * q + n + 1] for n in range(3)
            )
            level = level + (high + low * 2.0**-10) * jnp.exp2(power)
        norms.append(lax.rsqrt(level / (rows * cells) + 1e-06) * cells**-0.5)
    powers = [jnp.exp2(spare - TOP) for spare in spares]
    pair = 0
    for q in range(terms):
        for k in range(q, terms):
            here = slice(pair * own, (pair + 1) * own)
            total = parts[0][here, :]
            for part, power in zip(parts[1:], powers):
                total = total + part[here, :] * power[:, pair : pair + 1]
            out[:, pair, :] = total * (norms[q] * norms[k])
            pair += 1


def per_device(basis, slab_region, coef_index, coef_table):
    terms = coef_index.shape[1]
    rows, cells = basis.shape
    width = cells // slab_region.shape[0]
    count = lax.axis_size("mode")
    planes = count // GROUP
    own = rows // count
    lines = planes * own
    every = rows + lines
    pairs = terms * (terms + 1) // 2
    slabs = 2 * slab_region.shape[0]
    sizes = (rows, terms, own, planes)
    flops = 20_000_000_000

    chip = (shape((slabs, every, width), BF16), shape((slabs, KROWS, width), BF16))
    sums = (shape((pairs * lines, rows)), shape((terms, 8, width)))

    def scratch(number):
        return [
            pltpu.VMEM((every, 2 * width), F32),
            pltpu.VMEM((terms, rows, number * width), BF16),
            pltpu.VMEM((terms * lines, number * width), BF16),
        ]

    def ends(number, borders):
        return [pltpu.VMEM((number, every, width), BF16), pltpu.VMEM((borders, KROWS, width), BF16)]

    block = payload(basis, slab_region, coef_index, coef_table)
    by_x = flip(block, X, count)
    by_y = flip(block, Y, count)
    by_core = flip(block, CORE, count)
    field, weights, total, squares = call(
        functools.partial(own_kernel, *sizes), chip + sums, scratch(slabs - 2), flops=flops // 8
    )(block, by_core)
    by_x, by_y, total = lax.optimization_barrier((by_x, by_y, total))

    half = block.shape[0] // 2
    one = flip(by_x[:half], Y, count)
    two = flip(by_y[half:], X, count)
    by_xy_core = flip(jnp.concatenate([by_x, by_y], axis=0), CORE, count)
    strip = call(edge_kernel, shape((rows * width // cells, cells), BF16))(
        block, by_core, by_x, by_y
    )
    pairs_of = []
    for i in range(count):
        here = i % GROUP
        if here in (0, 1, 2, 4):
            to = (i - here - GROUP) % count + (6 if here == 1 else here)
        else:
            to = (i - here + GROUP) % count + (1 if here == 6 else here)
        pairs_of.append((i, to))
    strip = lax.ppermute(strip, "mode", pairs_of)
    x_field, x_weights, y_field, y_weights, total, squares = call(
        functools.partial(middle_kernel, *sizes),
        chip + chip + sums,
        scratch(2 * slabs - 2) + ends(4, 2),
        flops=flops // 4,
    )(by_x, by_y, by_xy_core, field, weights, total, squares)

    diagonal = flip(jnp.concatenate([one, two, strip], axis=0), CORE, count)
    high_rows = pairs * own + 8 - (pairs * own) % 8
    mine, others, levels = call(
        functools.partial(last_kernel, *sizes),
        (shape((high_rows, rows)), shape((planes - 1, high_rows, rows)), shape((8, 128))),
        [pltpu.VMEM(o.shape, o.dtype) for o in chip + sums] + scratch(slabs + 4) + ends(14, 6),
        flops=flops // 4,
    )(
        one, two, strip, diagonal, field, x_field, y_field, weights, x_weights, y_weights,
        total, squares,
    )

    parts = [mine]
    others = others.astype(jnp.float16)
    for z in range(1, planes):
        there = [(i, (i + z * GROUP) % count) for i in range(count)]
        parts.append(lax.ppermute(others[z - 1], "mode", there).astype(F32))
    out = call(
        functools.partial(finish_kernel, own, terms, cells * count), shape((own, pairs, rows))
    )(*parts, levels)
    return jnp.transpose(out, (1, 0, 2))


def solution(mesh):
    return jax.shard_map(
        per_device,
        mesh=mesh,
        in_specs=(P("groups", "mode"), P(("groups", "mode")), P("groups", None), P("groups")),
        out_specs=P(None, ("groups", "mode"), None),
        check_vma=False,
    )
```

```python
import functools

import jax
import jax.numpy as jnp
from jax import lax
from jax.experimental import pallas as pl
from jax.experimental.pallas import tpu as pltpu
from jax.sharding import PartitionSpec as P

GROUP = 8
CORE, X, Y = 1, 2, 4
KROWS = 32
TOP = 14.0
PAIR_LANES = 32
F32 = jnp.float32
BF16 = jnp.bfloat16
VMEM = pl.BlockSpec(memory_space=pltpu.VMEM)
HBM = pl.BlockSpec(memory_space=pltpu.HBM)


def call(kernel, outs, scratch=(), aliases=None, ins=None):
    def run(*args):
        return pl.pallas_call(
            kernel,
            out_shape=outs,
            in_specs=[VMEM] * len(args) if ins is None else ins,
            out_specs=jax.tree.map(lambda _: VMEM, outs),
            scratch_shapes=list(scratch),
            input_output_aliases=aliases or {},
            compiler_params=pltpu.CompilerParams(vmem_limit_bytes=32 * 1024 * 1024),
            cost_estimate=pl.CostEstimate(flops=0, bytes_accessed=0, transcendentals=0),
        )(*args)

    return run


def shape(dims, dtype=F32):
    return jax.ShapeDtypeStruct(dims, dtype)


def place():
    me = lax.axis_index("mode")
    return lax.rem(me, GROUP), lax.div(me, GROUP)


def flip(values, mask, count):
    return lax.ppermute(values, "mode", [(i, i ^ mask) for i in range(count)])


def weight_kernel(region, index, table, out, region_s, index_s, table_s, sems):
    copies = [
        pltpu.make_async_copy(region, region_s, sems.at[0]),
        pltpu.make_async_copy(index, index_s, sems.at[1]),
        pltpu.make_async_copy(table, table_s, sems.at[2]),
    ]
    for copy in copies:
        copy.start()
    for copy in copies:
        copy.wait()
    slabs = region.shape[0]
    width = out.shape[1] // slabs
    terms = index.shape[0]
    entries = table.shape[0]
    row = lax.broadcasted_iota(jnp.int32, (KROWS, width), 0)
    for s in range(slabs):
        reg = region_s[s]
        block = jnp.zeros((KROWS, width), F32)
        for q in range(terms):
            at = index_s[q, reg]
            kappa = jnp.where(at < entries, table_s[jnp.minimum(at, entries - 1)], 0.0)
            block = jnp.where(lax.div(row, 3) == q, kappa, block)
        high = block.astype(BF16).astype(F32)
        mid = (block - high).astype(BF16).astype(F32)
        low = block - high - mid
        part = lax.rem(row, 3)
        block = jnp.where(part == 0, high, jnp.where(part == 1, mid, low))
        out[:, s * width : (s + 1) * width] = block.astype(BF16)


def weight_rows(cells, region, index, table):
    return call(
        weight_kernel,
        shape((KROWS, cells), BF16),
        [
            pltpu.SMEM(region.shape, jnp.int32),
            pltpu.SMEM(index.shape[::-1], jnp.int32),
            pltpu.SMEM(table.shape, F32),
            pltpu.SemaphoreType.DMA((3,)),
        ],
        ins=[HBM] * 3,
    )(region, index.T, table)


def selector(own, rows, planes):
    j, a = place()
    line = lax.broadcasted_iota(jnp.int32, (planes * own, rows), 0)
    column = lax.broadcasted_iota(jnp.int32, (planes * own, rows), 1)
    shift = jnp.zeros((planes * own, rows), jnp.int32)
    for k in range(planes):
        start = lax.rem(a + k, planes) * (GROUP * own) + j * own - k * own
        shift = jnp.where(line >= k * own, start, shift)
    return jnp.where(column - line == shift, 1.0, 0.0).astype(BF16)


def across(width):
    line = lax.broadcasted_iota(jnp.int32, (width, width), 0)
    column = lax.broadcasted_iota(jnp.int32, (width, width), 1)
    same = jnp.where(line == column, 1.0, 0.0)
    beside = jnp.where(jnp.abs(line - column) == 1, 1.0, 0.0)
    mirror = jnp.where(line + column == width - 1, 1.0, 0.0)
    return jnp.concatenate([2.0 * same - beside, same - mirror], axis=1).astype(BF16)


def act(triples, stencil, side, right, left, squares, base, rows, terms):
    total, width = triples[0][1].shape
    own = total - rows
    for n, (before, here, after, weight) in enumerate(triples):
        lanes = pl.ds(base + n * width, width)
        side[...] = jnp.dot(here[...], stencil, preferred_element_type=F32)
        table = weight[...].astype(F32)
        kappas = []
        for q in range(terms):
            one = (table[3 * q : 3 * q + 1] + table[3 * q + 1 : 3 * q + 2]) + table[
                3 * q + 2 : 3 * q + 3
            ]
            kappas.append(jnp.broadcast_to(one, (8, width))[None])
        sums = [jnp.zeros((8, width), F32) for _ in range(terms)]
        for start in range(0, total, own):
            part = slice(start, start + own)
            value = here[part, :].astype(F32)
            back = value - before[part, :].astype(F32)
            ahead = value - after[part, :].astype(F32)
            shapes = (
                back + ahead,
                side[part, 0:width],
                back,
                ahead,
                side[part, width : 2 * width],
                value,
            )
            for q in range(terms):
                action = shapes[q].reshape(own // 8, 8, width) * kappas[q]
                action = action.reshape(own, width).astype(BF16)
                if start < rows:
                    right[q, part, lanes] = action
                    rounded = action.astype(F32).reshape(own // 8, 8, width)
                    sums[q] += jnp.sum(rounded * rounded, axis=0)
                else:
                    left[q * own : (q + 1) * own, lanes] = action
        for q in range(terms):
            squares[q] += sums[q]


def contract(left, right, total, own, terms, depth, before=None):
    offset = 0
    for k in range(terms):
        lines = own * (k + 1)
        product = lax.dot_general(
            left[0:lines, 0:depth],
            right[k, :, 0:depth],
            (((1,), (1,)), ((), ())),
            preferred_element_type=F32,
        )
        if before is not None:
            product = before[offset : offset + lines, :] + product
        total[offset : offset + lines, :] = product
        offset += lines


def spread(pieces, pick, field, weights, rows):
    j, _ = place()
    width = field.shape[2]
    for flipped, (table, *parts) in enumerate(pieces):
        core = jnp.bitwise_xor(jnp.bitwise_and(j, 1), flipped)
        slabs = table.shape[1] // width
        for s in range(slabs):
            lanes = slice(s * width, (s + 1) * width)
            at = core * slabs + s
            weights[at] = table[:, lanes]
            done = 0
            for part in parts:
                size = part.shape[0]
                field[at, done : done + size] = part[:, lanes]
                done += size
            field[at, rows:] = jnp.dot(
                pick, field[at, 0:rows], preferred_element_type=F32
            ).astype(BF16)


def split(ref, start, rows):
    return [ref.at[start + rows : start + rows + KROWS], ref.at[start : start + rows]]


def inner(field, weights, stencil, side, right, left, squares, base, rows, terms):
    slabs, _, width = field.shape

    @pl.loop(0, (slabs - 2) // 2)
    def _(t):
        s = 2 * t + 1
        triples = [
            (field.at[s + n - 1], field.at[s + n], field.at[s + n + 1], weights.at[s + n])
            for n in range(2)
        ]
        start = pl.multiple_of(base + 2 * t * width, width)
        act(triples, stencil, side, right, left, squares, start, rows, terms)


def pick_into(ends, at, field, slot, taken):
    @pl.when(taken)
    def _():
        ends[at] = field[slot]


def seam(ours, theirs, ends, seam_weights, field_weights, mine_first):
    slabs = ours.shape[0]
    for taken, (one, two) in (
        (mine_first, (0, 1)),
        (jnp.logical_not(mine_first), (1, 0)),
    ):

        @pl.when(taken)
        def _():
            fields = (ours, theirs)
            ends[0] = fields[one][slabs - 2]
            ends[1] = fields[one][slabs - 1]
            ends[2] = fields[two][0]
            ends[3] = fields[two][1]
            seam_weights[0] = field_weights[one][slabs - 1]
            seam_weights[1] = field_weights[two][0]


def own_kernel(rows, terms, own, planes, *refs):
    (mine, table, other, other_table,
     field, weights, total, squares, side, right, left) = refs
    squares[...] = jnp.zeros_like(squares)
    pick = selector(own, rows, planes)
    spread([[table, mine], [other_table, other]], pick, field, weights, rows)
    inner(field, weights, across(field.shape[2]), side, right, left, squares, 0, rows, terms)
    depth = (field.shape[0] - 2) * field.shape[2]
    contract(left, right, total, planes * own, terms, depth)


def row_kernel(rows, terms, own, planes, *refs):
    (mine, table, other, own_field, own_weights, total_in, squares_in,
     field, weights, total, squares, side, right, left, ends, end_weights) = refs
    j, _ = place()
    width = field.shape[2]
    stencil = across(width)
    squares[...] = squares_in[...]
    pick = selector(own, rows, planes)
    spread([[table, mine], split(other, 0, rows)], pick, field, weights, rows)
    depth = (field.shape[0] - 2) * width
    inner(field, weights, stencil, side, right, left, squares, 0, rows, terms)
    first = jnp.bitwise_and(j, X) == 0
    seam(own_field, field, ends, end_weights, (own_weights, weights), first)
    triples = [(ends.at[n], ends.at[n + 1], ends.at[n + 2], end_weights.at[n]) for n in range(2)]
    act(triples, stencil, side, right, left, squares, depth, rows, terms)
    contract(left, right, total, planes * own, terms, depth + 2 * width, total_in)


def lone_kernel(rows, terms, own, planes, *refs):
    (mine, table, other, total_in, squares_in,
     field, weights, total, squares, side, right, left) = refs
    squares[...] = squares_in[...]
    pick = selector(own, rows, planes)
    spread([[table, mine], split(other, rows + KROWS, rows)], pick, field, weights, rows)
    inner(field, weights, across(field.shape[2]), side, right, left, squares, 0, rows, terms)
    depth = (field.shape[0] - 2) * field.shape[2]
    contract(left, right, total, planes * own, terms, depth, total_in)


def edge_kernel(*refs):
    pieces, strip = refs[:-1], refs[-1]
    j, _ = place()
    lines, cells = strip.shape
    parts = pieces[0].shape[0] // lines
    width = cells // parts
    for piece, flips in zip(pieces, (0, CORE, X, Y)):
        for here, lanes in ((0, slice(0, width)), (GROUP - 1, slice(cells - width, cells))):

            @pl.when(jnp.bitwise_xor(j, flips) == here)
            def _():
                for n in range(parts):
                    strip[:, n * width : (n + 1) * width] = piece[
                        n * lines : (n + 1) * lines, lanes
                    ]


def last_kernel(rows, terms, own, planes, *refs):
    (one, two, strip, others_in, *rest) = refs
    fields, field_weights, rest = list(rest[:3]), list(rest[3:6]), rest[6:]
    (total_in, squares_in, mine, others, levels,
     field, weights, total, squares, side, right, left, ends, end_weights) = rest
    fields.append(field)
    field_weights.append(weights)
    slabs, every, width = field.shape
    lines = every - rows
    j, _ = place()
    chip = lax.div(j, 2)
    stencil = across(width)
    pick = selector(own, rows, planes)
    squares[...] = squares_in[...]
    height = one.shape[0] + two.shape[0]
    even = jnp.bitwise_and(j, CORE) == 0
    size = strip.shape[0]
    other = others_in[height:, :]
    first_core = jnp.where(even, strip[...], other)
    second_core = jnp.where(even, other, strip[...])
    for at, source in ((0, second_core), (5, first_core)):
        for n in range(rows // size):
            ends[at, n * size : (n + 1) * size] = source[:, n * width : (n + 1) * width]
        ends[at, rows:] = jnp.dot(pick, ends[at, 0:rows], preferred_element_type=F32).astype(BF16)
    part = one.shape[0] - KROWS
    there = others_in.at
    spread(
        [
            [one.at[part:], one.at[0:part], two],
            [there[part : part + KROWS], there[0:part], there[part + KROWS : height]],
        ],
        pick,
        field,
        weights,
        rows,
    )
    inner(field, weights, stencil, side, right, left, squares, 0, rows, terms)
    for n, source in enumerate(fields):
        for number, at, slots, weight in (
            (0, 1, (0, 1), 0),
            (3, 3, (slabs - 2, slabs - 1), 1),
            (1, 6, (slabs - 2, slabs - 1), 2),
            (2, 8, (0, 1), 3),
        ):

            @pl.when(jnp.bitwise_xor(chip, n) == number)
            def _():
                ends[at] = source[slots[0]]
                ends[at + 1] = source[slots[1]]
                end_weights[weight] = field_weights[n][slots[1] if slots[0] else 0]

    first = jnp.bitwise_and(j, X) == 0
    seam(fields[2], field, ends.at[10:14], end_weights.at[4:6], (field_weights[2], weights), first)
    triples = [
        (ends.at[n - 1], ends.at[n], ends.at[n + 1], end_weights.at[m])
        for m, n in enumerate((1, 4, 7, 8, 11, 12))
    ]
    depth = (slabs - 2) * width
    for n in range(0, 6, 2):
        act(triples[n : n + 2], stencil, side, right, left, squares, depth + n * width, rows, terms)
    contract(left, right, total, lines, terms, depth + 6 * width, total_in)
    lane = lax.broadcasted_iota(jnp.int32, (8, rows), 1)
    line = lax.broadcasted_iota(jnp.int32, (8, rows), 0)
    spare = jnp.zeros((8, rows), F32)
    for q in range(terms):
        level = jnp.sum(squares[q], keepdims=True)
        levels[q : q + 1, :] = jnp.broadcast_to(level, (1, levels.shape[1]))
        power = jnp.ceil(jnp.log2(jnp.maximum(level, 1e-30)))
        level = level * jnp.exp2(-power)
        high = jnp.floor(level * 2.0**10) * 2.0**-10
        low = (level - high) * 2.0**10
        low = jnp.floor(low * 2.0**10) * 2.0**-10
        for n, value in enumerate((power, high, low)):
            here = jnp.logical_and(line == 0, lane == PAIR_LANES + 3 * q + n)
            spare = jnp.where(here, value, spare)
    levels[terms:, :] = jnp.zeros((levels.shape[0] - terms, levels.shape[1]), F32)
    offset = 0
    for k in range(terms):
        for q in range(k + 1):
            pair = q * terms - q * (q - 1) // 2 + k - q
            at = offset + q * lines
            block = total[at : at + lines, :]
            largest = jnp.max(jnp.abs(block), keepdims=True)
            power = jnp.ceil(jnp.log2(jnp.maximum(largest, 1e-30)))
            spare = jnp.where(jnp.logical_and(line == 0, lane == pair), power, spare)
            scale = jnp.exp2(TOP - power)
            for z in range(planes):
                part = total[at + z * own : at + (z + 1) * own, :]
                if z == 0:
                    mine[pair * own : (pair + 1) * own, :] = part
                else:
                    others[z - 1, pair * own : (pair + 1) * own, :] = part * scale
        offset += (k + 1) * lines
    end = terms * (terms + 1) // 2 * own
    for z in range(1, planes):
        others[z - 1, end:, :] = spare[0 : others.shape[1] - end]


def finish_kernel(own, terms, cells, *refs):
    parts, (levels, out) = refs[:-2], refs[-2:]
    rows = parts[0].shape[1]
    pairs = terms * (terms + 1) // 2
    spares = [part[pairs * own : pairs * own + 1, 0:128] for part in parts[1:]]
    norms = []
    for q in range(terms):
        level = levels[q : q + 1, 0:1]
        for spare in spares:
            power, high, low = (
                spare[:, PAIR_LANES + 3 * q + n : PAIR_LANES + 3 * q + n + 1] for n in range(3)
            )
            level = level + (high + low * 2.0**-10) * jnp.exp2(power)
        norms.append(lax.rsqrt(level / (rows * cells) + 1e-06) * cells**-0.5)
    powers = [jnp.exp2(spare - TOP) for spare in spares]
    pair = 0
    for q in range(terms):
        for k in range(q, terms):
            here = slice(pair * own, (pair + 1) * own)
            total = parts[0][here, :]
            for part, power in zip(parts[1:], powers):
                total = total + part[here, :] * power[:, pair : pair + 1]
            out[:, pair, :] = total * (norms[q] * norms[k])
            pair += 1


def per_device(basis, slab_region, coef_index, coef_table):
    terms = coef_index.shape[1]
    rows, cells = basis.shape
    width = cells // slab_region.shape[0]
    count = lax.axis_size("mode")
    planes = count // GROUP
    own = rows // count
    lines = planes * own
    every = rows + lines
    pairs = terms * (terms + 1) // 2
    slabs = 2 * slab_region.shape[0]
    sizes = (rows, terms, own, planes)

    chip = (shape((slabs, every, width), BF16), shape((slabs, KROWS, width), BF16))
    sums = (shape((pairs * lines, rows)), shape((terms, 8, width)))

    def scratch(number):
        return [
            pltpu.VMEM((every, 2 * width), F32),
            pltpu.VMEM((terms, rows, number * width), BF16),
            pltpu.VMEM((terms * lines, number * width), BF16),
        ]

    def ends(number, borders):
        return [pltpu.VMEM((number, every, width), BF16), pltpu.VMEM((borders, KROWS, width), BF16)]

    by_x = flip(basis, X, count)
    by_y = flip(basis, Y, count)
    by_core = flip(basis, CORE, count)
    by_core, slab_region = lax.optimization_barrier((by_core, slab_region))
    table = weight_rows(cells, slab_region, coef_index, coef_table)
    table_core = flip(table, CORE, count)
    table_x = flip(table, X, count)
    table_y = flip(table, Y, count)
    field, weights, total, squares = call(
        functools.partial(own_kernel, *sizes), chip + sums, scratch(slabs - 2)
    )(basis, table, by_core, table_core)
    by_x, by_y, table_x, table_y, total = lax.optimization_barrier(
        (by_x, by_y, table_x, table_y, total)
    )

    half = (rows - KROWS) // 2
    one = flip(jnp.concatenate([by_x[:half], table_x], axis=0), Y, count)
    two = flip(by_y[half:], X, count)
    others = flip(jnp.concatenate([by_x, table_x, by_y, table_y], axis=0), CORE, count)
    strip = call(edge_kernel, shape((rows * width // cells, cells), BF16))(
        basis, by_core, by_x, by_y
    )
    pairs_of = []
    for i in range(count):
        here = i % GROUP
        if here in (0, 1, 2, 4):
            to = (i - here - GROUP) % count + (6 if here == 1 else here)
        else:
            to = (i - here + GROUP) % count + (1 if here == 6 else here)
        pairs_of.append((i, to))
    strip = lax.ppermute(strip, "mode", pairs_of)
    x_field, x_weights, total, squares = call(
        functools.partial(row_kernel, *sizes),
        chip + sums,
        scratch(slabs) + ends(4, 2),
    )(by_x, table_x, others, field, weights, total, squares)
    one, two, strip, total = lax.optimization_barrier((one, two, strip, total))

    diagonal = flip(jnp.concatenate([one, two, strip], axis=0), CORE, count)
    y_field, y_weights, total, squares = call(
        functools.partial(lone_kernel, *sizes), chip + sums, scratch(slabs - 2)
    )(by_y, table_y, others, total, squares)
    diagonal, total = lax.optimization_barrier((diagonal, total))

    high_rows = pairs * own + 8 - (pairs * own) % 8
    mine, others, levels = call(
        functools.partial(last_kernel, *sizes),
        (shape((high_rows, rows)), shape((planes - 1, high_rows, rows)), shape((8, 128))),
        [pltpu.VMEM(o.shape, o.dtype) for o in chip + sums] + scratch(slabs + 4) + ends(14, 6),
    )(
        one, two, strip, diagonal, field, x_field, y_field, weights, x_weights, y_weights,
        total, squares,
    )

    parts = [mine]
    others = others.astype(jnp.float16)
    for z in range(1, planes):
        there = [(i, (i + z * GROUP) % count) for i in range(count)]
        parts.append(lax.ppermute(others[z - 1], "mode", there).astype(F32))
    out = call(
        functools.partial(finish_kernel, own, terms, cells * count), shape((own, pairs, rows))
    )(*parts, levels)
    return jnp.transpose(out, (1, 0, 2))


def solution(mesh):
    return jax.shard_map(
        per_device,
        mesh=mesh,
        in_specs=(P("groups", "mode"), P(("groups", "mode")), P("groups", None), P("groups")),
        out_specs=P(None, ("groups", "mode"), None),
        check_vma=False,
    )
```

```python
import functools

import jax
import jax.numpy as jnp
from jax import lax
from jax.experimental import pallas as pl
from jax.experimental.pallas import tpu as pltpu
from jax.sharding import PartitionSpec as P

GROUP = 8
CORE, X, Y = 1, 2, 4
KROWS = 32
TOP = 14.0
PAIR_LANES = 32
F32 = jnp.float32
BF16 = jnp.bfloat16
VMEM = pl.BlockSpec(memory_space=pltpu.VMEM)
HBM = pl.BlockSpec(memory_space=pltpu.HBM)


def call(kernel, outs, scratch=(), aliases=None, ins=None):
    def run(*args):
        return pl.pallas_call(
            kernel,
            out_shape=outs,
            in_specs=[VMEM] * len(args) if ins is None else ins,
            out_specs=jax.tree.map(lambda _: VMEM, outs),
            scratch_shapes=list(scratch),
            input_output_aliases=aliases or {},
            compiler_params=pltpu.CompilerParams(vmem_limit_bytes=32 * 1024 * 1024),
            cost_estimate=pl.CostEstimate(flops=0, bytes_accessed=0, transcendentals=0),
        )(*args)

    return run


def shape(dims, dtype=F32):
    return jax.ShapeDtypeStruct(dims, dtype)


def place():
    me = lax.axis_index("mode")
    return lax.rem(me, GROUP), lax.div(me, GROUP)


def flip(values, mask, count):
    return lax.ppermute(values, "mode", [(i, i ^ mask) for i in range(count)])


def weight_kernel(region, index, table, out, region_s, index_s, table_s, sems):
    copies = [
        pltpu.make_async_copy(region, region_s, sems.at[0]),
        pltpu.make_async_copy(index, index_s, sems.at[1]),
        pltpu.make_async_copy(table, table_s, sems.at[2]),
    ]
    for copy in copies:
        copy.start()
    for copy in copies:
        copy.wait()
    slabs = region.shape[0]
    width = out.shape[1] // slabs
    terms = index.shape[0]
    entries = table.shape[0]
    row = lax.broadcasted_iota(jnp.int32, (KROWS, width), 0)
    for s in range(slabs):
        reg = region_s[s]
        block = jnp.zeros((KROWS, width), F32)
        for q in range(terms):
            at = index_s[q, reg]
            kappa = jnp.where(at < entries, table_s[jnp.minimum(at, entries - 1)], 0.0)
            block = jnp.where(lax.div(row, 3) == q, kappa, block)
        high = block.astype(BF16).astype(F32)
        mid = (block - high).astype(BF16).astype(F32)
        low = block - high - mid
        part = lax.rem(row, 3)
        block = jnp.where(part == 0, high, jnp.where(part == 1, mid, low))
        out[:, s * width : (s + 1) * width] = block.astype(BF16)


def weight_rows(cells, region, index, table):
    return call(
        weight_kernel,
        shape((KROWS, cells), BF16),
        [
            pltpu.SMEM(region.shape, jnp.int32),
            pltpu.SMEM(index.shape[::-1], jnp.int32),
            pltpu.SMEM(table.shape, F32),
            pltpu.SemaphoreType.DMA((3,)),
        ],
        ins=[HBM] * 3,
    )(region, index.T, table)


def selector(own, rows, planes):
    j, a = place()
    line = lax.broadcasted_iota(jnp.int32, (planes * own, rows), 0)
    column = lax.broadcasted_iota(jnp.int32, (planes * own, rows), 1)
    shift = jnp.zeros((planes * own, rows), jnp.int32)
    for k in range(planes):
        start = lax.rem(a + k, planes) * (GROUP * own) + j * own - k * own
        shift = jnp.where(line >= k * own, start, shift)
    return jnp.where(column - line == shift, 1.0, 0.0).astype(BF16)


def across(width):
    line = lax.broadcasted_iota(jnp.int32, (width, width), 0)
    column = lax.broadcasted_iota(jnp.int32, (width, width), 1)
    same = jnp.where(line == column, 1.0, 0.0)
    beside = jnp.where(jnp.abs(line - column) == 1, 1.0, 0.0)
    mirror = jnp.where(line + column == width - 1, 1.0, 0.0)
    return jnp.concatenate([2.0 * same - beside, same - mirror], axis=1).astype(BF16)


def act(triples, stencil, sides, right, left, squares, base, rows, terms):
    total, width = triples[0][1].shape
    own = total - rows
    for n, (before, here, after, weight) in enumerate(triples):
        lanes = slice(base + n * width, base + (n + 1) * width)
        side = sides.at[n % 2]
        side[...] = jnp.dot(here[...], stencil, preferred_element_type=F32)
        table = weight[...].astype(F32)
        kappas = []
        for q in range(terms):
            one = (table[3 * q : 3 * q + 1] + table[3 * q + 1 : 3 * q + 2]) + table[
                3 * q + 2 : 3 * q + 3
            ]
            kappas.append(jnp.broadcast_to(one, (8, width))[None])
        sums = [jnp.zeros((8, width), F32) for _ in range(terms)]
        for start in range(0, total, own):
            part = slice(start, start + own)
            value = here[part, :].astype(F32)
            back = value - before[part, :].astype(F32)
            ahead = value - after[part, :].astype(F32)
            shapes = (
                back + ahead,
                side[part, 0:width],
                back,
                ahead,
                side[part, width : 2 * width],
                value,
            )
            for q in range(terms):
                action = shapes[q].reshape(own // 8, 8, width) * kappas[q]
                action = action.reshape(own, width).astype(BF16)
                if start < rows:
                    right[q, part, lanes] = action
                    rounded = action.astype(F32).reshape(own // 8, 8, width)
                    sums[q] += jnp.sum(rounded * rounded, axis=0)
                else:
                    left[q * own : (q + 1) * own, lanes] = action
        for q in range(terms):
            squares[q] += sums[q]


def contract(left, right, total, own, terms, depth, before=None):
    offset = 0
    for k in range(terms):
        lines = own * (k + 1)
        product = lax.dot_general(
            left[0:lines, 0:depth],
            right[k, :, 0:depth],
            (((1,), (1,)), ((), ())),
            preferred_element_type=F32,
        )
        if before is not None:
            product = before[offset : offset + lines, :] + product
        total[offset : offset + lines, :] = product
        offset += lines


def spread(pieces, pick, field, weights, rows):
    j, _ = place()
    width = field.shape[2]
    for flipped, (table, *parts) in enumerate(pieces):
        core = jnp.bitwise_xor(jnp.bitwise_and(j, 1), flipped)
        slabs = table.shape[1] // width
        block = jnp.concatenate([part[...] for part in parts], axis=0)
        picked = jnp.dot(pick, block, preferred_element_type=F32).astype(BF16)
        for s in range(slabs):
            lanes = slice(s * width, (s + 1) * width)
            at = core * slabs + s
            weights[at] = table[:, lanes]
            done = 0
            for part in parts:
                size = part.shape[0]
                field[at, done : done + size] = part[:, lanes]
                done += size
            field[at, rows:] = picked[:, lanes]


def split(ref, start, rows):
    return [ref.at[start + rows : start + rows + KROWS], ref.at[start : start + rows]]


def inner(field, weights, stencil, side, right, left, squares, base, rows, terms):
    triples = [
        (field.at[s - 1], field.at[s], field.at[s + 1], weights.at[s])
        for s in range(1, field.shape[0] - 1)
    ]
    act(triples, stencil, side, right, left, squares, base, rows, terms)


def seam(ours, theirs, ends, seam_weights, field_weights, mine_first):
    slabs = ours.shape[0]
    for taken, (one, two) in (
        (mine_first, (0, 1)),
        (jnp.logical_not(mine_first), (1, 0)),
    ):

        @pl.when(taken)
        def _():
            fields = (ours, theirs)
            ends[0] = fields[one][slabs - 2]
            ends[1] = fields[one][slabs - 1]
            ends[2] = fields[two][0]
            ends[3] = fields[two][1]
            seam_weights[0] = field_weights[one][slabs - 1]
            seam_weights[1] = field_weights[two][0]


def own_kernel(rows, terms, own, planes, *refs):
    (mine, table, other, other_table,
     field, weights, total, squares, side, right, left) = refs
    squares[...] = jnp.zeros_like(squares)
    pick = selector(own, rows, planes)
    spread([[table, mine], [other_table, other]], pick, field, weights, rows)
    inner(field, weights, across(field.shape[2]), side, right, left, squares, 0, rows, terms)
    depth = (field.shape[0] - 2) * field.shape[2]
    contract(left, right, total, planes * own, terms, depth)


def row_kernel(rows, terms, own, planes, *refs):
    (mine, table, other, own_field, own_weights, total_in, squares_in,
     field, weights, total, squares, side, right, left, ends, end_weights) = refs
    j, _ = place()
    width = field.shape[2]
    stencil = across(width)
    squares[...] = squares_in[...]
    pick = selector(own, rows, planes)
    spread([[table, mine], split(other, 0, rows)], pick, field, weights, rows)
    depth = (field.shape[0] - 2) * width
    inner(field, weights, stencil, side, right, left, squares, 0, rows, terms)
    first = jnp.bitwise_and(j, X) == 0
    seam(own_field, field, ends, end_weights, (own_weights, weights), first)
    triples = [(ends.at[n], ends.at[n + 1], ends.at[n + 2], end_weights.at[n]) for n in range(2)]
    act(triples, stencil, side, right, left, squares, depth, rows, terms)
    contract(left, right, total, planes * own, terms, depth + 2 * width, total_in)


def lone_kernel(rows, terms, own, planes, *refs):
    (mine, table, other, total_in, squares_in,
     field, weights, total, squares, side, right, left) = refs
    squares[...] = squares_in[...]
    pick = selector(own, rows, planes)
    spread([[table, mine], split(other, rows + KROWS, rows)], pick, field, weights, rows)
    inner(field, weights, across(field.shape[2]), side, right, left, squares, 0, rows, terms)
    depth = (field.shape[0] - 2) * field.shape[2]
    contract(left, right, total, planes * own, terms, depth, total_in)


def edge_kernel(*refs):
    pieces, strip = refs[:-1], refs[-1]
    j, _ = place()
    lines, cells = strip.shape
    parts = pieces[0].shape[0] // lines
    width = cells // parts
    for piece, flips in zip(pieces, (0, CORE, X, Y)):
        for here, lanes in ((0, slice(0, width)), (GROUP - 1, slice(cells - width, cells))):

            @pl.when(jnp.bitwise_xor(j, flips) == here)
            def _():
                for n in range(parts):
                    strip[:, n * width : (n + 1) * width] = piece[
                        n * lines : (n + 1) * lines, lanes
                    ]


def last_kernel(rows, terms, own, planes, *refs):
    (one, two, strip, others_in, *rest) = refs
    fields, field_weights, rest = list(rest[:3]), list(rest[3:6]), rest[6:]
    (total_in, squares_in, mine, others, levels,
     field, weights, total, squares, side, right, left, ends, end_weights) = rest
    fields.append(field)
    field_weights.append(weights)
    slabs, every, width = field.shape
    lines = every - rows
    j, _ = place()
    chip = lax.div(j, 2)
    stencil = across(width)
    pick = selector(own, rows, planes)
    squares[...] = squares_in[...]
    height = one.shape[0] + two.shape[0]
    even = jnp.bitwise_and(j, CORE) == 0
    size = strip.shape[0]
    other = others_in[height:, :]
    first_core = jnp.where(even, strip[...], other)
    second_core = jnp.where(even, other, strip[...])
    for at, source in ((0, second_core), (5, first_core)):
        for n in range(rows // size):
            ends[at, n * size : (n + 1) * size] = source[:, n * width : (n + 1) * width]
        ends[at, rows:] = jnp.dot(pick, ends[at, 0:rows], preferred_element_type=F32).astype(BF16)
    part = one.shape[0] - KROWS
    there = others_in.at
    spread(
        [
            [one.at[part:], one.at[0:part], two],
            [there[part : part + KROWS], there[0:part], there[part + KROWS : height]],
        ],
        pick,
        field,
        weights,
        rows,
    )
    inner(field, weights, stencil, side, right, left, squares, 0, rows, terms)
    for n, source in enumerate(fields):
        for number, at, slots, weight in (
            (0, 1, (0, 1), 0),
            (3, 3, (slabs - 2, slabs - 1), 1),
            (1, 6, (slabs - 2, slabs - 1), 2),
            (2, 8, (0, 1), 3),
        ):

            @pl.when(jnp.bitwise_xor(chip, n) == number)
            def _():
                ends[at] = source[slots[0]]
                ends[at + 1] = source[slots[1]]
                end_weights[weight] = field_weights[n][slots[1] if slots[0] else 0]

    first = jnp.bitwise_and(j, X) == 0
    seam(fields[2], field, ends.at[10:14], end_weights.at[4:6], (field_weights[2], weights), first)
    triples = [
        (ends.at[n - 1], ends.at[n], ends.at[n + 1], end_weights.at[m])
        for m, n in enumerate((1, 4, 7, 8, 11, 12))
    ]
    depth = (slabs - 2) * width
    for n in range(0, 6, 2):
        act(triples[n : n + 2], stencil, side, right, left, squares, depth + n * width, rows, terms)
    contract(left, right, total, lines, terms, depth + 6 * width, total_in)
    lane = lax.broadcasted_iota(jnp.int32, (8, rows), 1)
    line = lax.broadcasted_iota(jnp.int32, (8, rows), 0)
    spare = jnp.zeros((8, rows), F32)
    for q in range(terms):
        level = jnp.sum(squares[q], keepdims=True)
        levels[q : q + 1, :] = jnp.broadcast_to(level, (1, levels.shape[1]))
        power = jnp.ceil(jnp.log2(jnp.maximum(level, 1e-30)))
        level = level * jnp.exp2(-power)
        high = jnp.floor(level * 2.0**10) * 2.0**-10
        low = (level - high) * 2.0**10
        low = jnp.floor(low * 2.0**10) * 2.0**-10
        for n, value in enumerate((power, high, low)):
            here = jnp.logical_and(line == 0, lane == PAIR_LANES + 3 * q + n)
            spare = jnp.where(here, value, spare)
    levels[terms:, :] = jnp.zeros((levels.shape[0] - terms, levels.shape[1]), F32)
    offset = 0
    for k in range(terms):
        for q in range(k + 1):
            pair = q * terms - q * (q - 1) // 2 + k - q
            at = offset + q * lines
            block = total[at : at + lines, :]
            largest = jnp.max(jnp.abs(block), keepdims=True)
            power = jnp.ceil(jnp.log2(jnp.maximum(largest, 1e-30)))
            spare = jnp.where(jnp.logical_and(line == 0, lane == pair), power, spare)
            scale = jnp.exp2(TOP - power)
            for z in range(planes):
                part = total[at + z * own : at + (z + 1) * own, :]
                if z == 0:
                    mine[pair * own : (pair + 1) * own, :] = part
                else:
                    others[z - 1, pair * own : (pair + 1) * own, :] = part * scale
        offset += (k + 1) * lines
    end = terms * (terms + 1) // 2 * own
    for z in range(1, planes):
        others[z - 1, end:, :] = spare[0 : others.shape[1] - end]


def finish_kernel(own, terms, cells, *refs):
    parts, (levels, out) = refs[:-2], refs[-2:]
    rows = parts[0].shape[1]
    pairs = terms * (terms + 1) // 2
    spares = [part[pairs * own : pairs * own + 1, 0:128] for part in parts[1:]]
    norms = []
    for q in range(terms):
        level = levels[q : q + 1, 0:1]
        for spare in spares:
            power, high, low = (
                spare[:, PAIR_LANES + 3 * q + n : PAIR_LANES + 3 * q + n + 1] for n in range(3)
            )
            level = level + (high + low * 2.0**-10) * jnp.exp2(power)
        norms.append(lax.rsqrt(level / (rows * cells) + 1e-06) * cells**-0.5)
    powers = [jnp.exp2(spare - TOP) for spare in spares]
    pair = 0
    for q in range(terms):
        for k in range(q, terms):
            here = slice(pair * own, (pair + 1) * own)
            total = parts[0][here, :]
            for part, power in zip(parts[1:], powers):
                total = total + part[here, :] * power[:, pair : pair + 1]
            out[:, pair, :] = total * (norms[q] * norms[k])
            pair += 1


def per_device(basis, slab_region, coef_index, coef_table):
    terms = coef_index.shape[1]
    rows, cells = basis.shape
    width = cells // slab_region.shape[0]
    count = lax.axis_size("mode")
    planes = count // GROUP
    own = rows // count
    lines = planes * own
    every = rows + lines
    pairs = terms * (terms + 1) // 2
    slabs = 2 * slab_region.shape[0]
    sizes = (rows, terms, own, planes)

    chip = (shape((slabs, every, width), BF16), shape((slabs, KROWS, width), BF16))
    sums = (shape((pairs * lines, rows)), shape((terms, 8, width)))

    def scratch(number):
        return [
            pltpu.VMEM((2, every, 2 * width), F32),
            pltpu.VMEM((terms, rows, number * width), BF16),
            pltpu.VMEM((terms * lines, number * width), BF16),
        ]

    def ends(number, borders):
        return [pltpu.VMEM((number, every, width), BF16), pltpu.VMEM((borders, KROWS, width), BF16)]

    by_x = flip(basis, X, count)
    by_y = flip(basis, Y, count)
    by_core = flip(basis, CORE, count)
    by_core, slab_region = lax.optimization_barrier((by_core, slab_region))
    table = weight_rows(cells, slab_region, coef_index, coef_table)
    table_core = flip(table, CORE, count)
    table_x = flip(table, X, count)
    table_y = flip(table, Y, count)
    field, weights, total, squares = call(
        functools.partial(own_kernel, *sizes), chip + sums, scratch(slabs - 2)
    )(basis, table, by_core, table_core)
    by_x, by_y, table_x, table_y, total = lax.optimization_barrier(
        (by_x, by_y, table_x, table_y, total)
    )

    half = (rows - KROWS) // 2
    one = flip(jnp.concatenate([by_x[:half], table_x], axis=0), Y, count)
    two = flip(by_y[half:], X, count)
    others = flip(jnp.concatenate([by_x, table_x, by_y, table_y], axis=0), CORE, count)
    strip = call(edge_kernel, shape((rows * width // cells, cells), BF16))(
        basis, by_core, by_x, by_y
    )
    pairs_of = []
    for i in range(count):
        here = i % GROUP
        if here in (0, 1, 2, 4):
            to = (i - here - GROUP) % count + (6 if here == 1 else here)
        else:
            to = (i - here + GROUP) % count + (1 if here == 6 else here)
        pairs_of.append((i, to))
    strip = lax.ppermute(strip, "mode", pairs_of)
    x_field, x_weights, total, squares = call(
        functools.partial(row_kernel, *sizes),
        chip + sums,
        scratch(slabs) + ends(4, 2),
    )(by_x, table_x, others, field, weights, total, squares)
    one, two, strip, total = lax.optimization_barrier((one, two, strip, total))

    diagonal = flip(jnp.concatenate([one, two, strip], axis=0), CORE, count)
    y_field, y_weights, total, squares = call(
        functools.partial(lone_kernel, *sizes), chip + sums, scratch(slabs - 2)
    )(by_y, table_y, others, total, squares)
    diagonal, total = lax.optimization_barrier((diagonal, total))

    high_rows = pairs * own + 8 - (pairs * own) % 8
    mine, others, levels = call(
        functools.partial(last_kernel, *sizes),
        (shape((high_rows, rows)), shape((planes - 1, high_rows, rows)), shape((8, 128))),
        [pltpu.VMEM(o.shape, o.dtype) for o in chip + sums] + scratch(slabs + 4) + ends(14, 6),
    )(
        one, two, strip, diagonal, field, x_field, y_field, weights, x_weights, y_weights,
        total, squares,
    )

    parts = [mine]
    others = others.astype(jnp.float16)
    for z in range(1, planes):
        there = [(i, (i + z * GROUP) % count) for i in range(count)]
        parts.append(lax.ppermute(others[z - 1], "mode", there).astype(F32))
    out = call(
        functools.partial(finish_kernel, own, terms, cells * count), shape((own, pairs, rows))
    )(*parts, levels)
    return jnp.transpose(out, (1, 0, 2))


def solution(mesh):
    return jax.shard_map(
        per_device,
        mesh=mesh,
        in_specs=(P("groups", "mode"), P(("groups", "mode")), P("groups", None), P("groups")),
        out_specs=P(None, ("groups", "mode"), None),
        check_vma=False,
    )
```

```python
import functools

import jax
import jax.numpy as jnp
from jax import lax
from jax.experimental import pallas as pl
from jax.experimental.pallas import tpu as pltpu
from jax.sharding import PartitionSpec as P

GROUP = 8
CORE, X, Y = 1, 2, 4
KROWS = 32
TOP = 14.0
F32 = jnp.float32
BF16 = jnp.bfloat16
VMEM = pl.BlockSpec(memory_space=pltpu.VMEM)
HBM = pl.BlockSpec(memory_space=pltpu.HBM)


def call(kernel, outs, scratch=(), aliases=None, ins=None):
    def run(*args):
        return pl.pallas_call(
            kernel,
            out_shape=outs,
            in_specs=[VMEM] * len(args) if ins is None else ins,
            out_specs=jax.tree.map(lambda _: VMEM, outs),
            scratch_shapes=list(scratch),
            input_output_aliases=aliases or {},
            compiler_params=pltpu.CompilerParams(vmem_limit_bytes=32 * 1024 * 1024),
            cost_estimate=pl.CostEstimate(flops=0, bytes_accessed=0, transcendentals=0),
        )(*args)

    return run


def shape(dims, dtype=F32):
    return jax.ShapeDtypeStruct(dims, dtype)


def place():
    me = lax.axis_index("mode")
    return lax.rem(me, GROUP), lax.div(me, GROUP)


def flip(values, mask, count):
    return lax.ppermute(values, "mode", [(i, i ^ mask) for i in range(count)])


def weight_kernel(region, index, table, out, region_s, index_s, table_s, sems):
    copies = [
        pltpu.make_async_copy(region, region_s, sems.at[0]),
        pltpu.make_async_copy(index, index_s, sems.at[1]),
        pltpu.make_async_copy(table, table_s, sems.at[2]),
    ]
    for copy in copies:
        copy.start()
    for copy in copies:
        copy.wait()
    slabs = region.shape[0]
    width = out.shape[1] // slabs
    terms = index.shape[0]
    entries = table.shape[0]
    row = lax.broadcasted_iota(jnp.int32, (KROWS, width), 0)
    for s in range(slabs):
        reg = region_s[s]
        block = jnp.zeros((KROWS, width), F32)
        for q in range(terms):
            at = index_s[q, reg]
            kappa = jnp.where(at < entries, table_s[jnp.minimum(at, entries - 1)], 0.0)
            block = jnp.where(lax.div(row, 3) == q, kappa, block)
        high = block.astype(BF16).astype(F32)
        mid = (block - high).astype(BF16).astype(F32)
        low = block - high - mid
        part = lax.rem(row, 3)
        block = jnp.where(part == 0, high, jnp.where(part == 1, mid, low))
        out[:, s * width : (s + 1) * width] = block.astype(BF16)


def weight_rows(cells, region, index, table):
    return call(
        weight_kernel,
        shape((KROWS, cells), BF16),
        [
            pltpu.SMEM(region.shape, jnp.int32),
            pltpu.SMEM(index.shape[::-1], jnp.int32),
            pltpu.SMEM(table.shape, F32),
            pltpu.SemaphoreType.DMA((3,)),
        ],
        ins=[HBM] * 3,
    )(region, index.T, table)


def selector(own, rows, planes):
    j, a = place()
    line = lax.broadcasted_iota(jnp.int32, (planes * own, rows), 0)
    column = lax.broadcasted_iota(jnp.int32, (planes * own, rows), 1)
    shift = jnp.zeros((planes * own, rows), jnp.int32)
    for k in range(planes):
        start = lax.rem(a + k, planes) * (GROUP * own) + j * own - k * own
        shift = jnp.where(line >= k * own, start, shift)
    return jnp.where(column - line == shift, 1.0, 0.0).astype(BF16)


def across(width):
    line = lax.broadcasted_iota(jnp.int32, (width, width), 0)
    column = lax.broadcasted_iota(jnp.int32, (width, width), 1)
    same = jnp.where(line == column, 1.0, 0.0)
    beside = jnp.where(jnp.abs(line - column) == 1, 1.0, 0.0)
    mirror = jnp.where(line + column == width - 1, 1.0, 0.0)
    return jnp.concatenate([2.0 * same - beside, same - mirror], axis=1).astype(BF16)


def act(triples, stencil, sides, right, left, squares, rows, terms):
    total, width = triples[0][1].shape
    own = total - rows
    for n, (before, here, after, weight) in enumerate(triples):
        lanes = slice(n * width, (n + 1) * width)
        side = sides.at[n % 2]
        side[...] = jnp.dot(here[...], stencil, preferred_element_type=F32)
        table = weight[...].astype(F32)
        kappas = []
        for q in range(terms):
            one = (table[3 * q : 3 * q + 1] + table[3 * q + 1 : 3 * q + 2]) + table[
                3 * q + 2 : 3 * q + 3
            ]
            kappas.append(jnp.broadcast_to(one, (8, width))[None])
        sums = [jnp.zeros((8, width), F32) for _ in range(terms)]
        for start in range(0, total, own):
            part = slice(start, start + own)
            value = here[part, :].astype(F32)
            back = value - before[part, :].astype(F32)
            ahead = value - after[part, :].astype(F32)
            shapes = (
                back + ahead,
                side[part, 0:width],
                back,
                ahead,
                side[part, width : 2 * width],
                value,
            )
            for q in range(terms):
                action = shapes[q].reshape(own // 8, 8, width) * kappas[q]
                action = action.reshape(own, width).astype(BF16)
                if start < rows:
                    right[q, part, lanes] = action
                    rounded = action.astype(F32).reshape(own // 8, 8, width)
                    sums[q] += jnp.sum(rounded * rounded, axis=0)
                else:
                    left[q * own : (q + 1) * own, lanes] = action
        for q in range(terms):
            squares[q] += sums[q]


def contract(left, right, own, terms, depth, before, store):
    offset = 0
    for k in range(terms):
        lines = own * (k + 1)
        product = lax.dot_general(
            left[0:lines, 0:depth],
            right[k, :, 0:depth],
            (((1,), (1,)), ((), ())),
            preferred_element_type=F32,
        )
        if before is not None:
            product = before[offset : offset + lines, :] + product
        store(offset, k, product)
        offset += lines


def keep(total):
    def store(offset, _, product):
        total[offset : offset + product.shape[0], :] = product

    return store


def spread(chip, pieces, pick, field, weights, rows):
    j, _ = place()
    width = field.shape[2]
    for flipped, (table, *parts) in enumerate(pieces):
        core = jnp.bitwise_xor(jnp.bitwise_and(j, 1), flipped)
        slabs = table.shape[1] // width
        block = jnp.concatenate([part[...] for part in parts], axis=0)
        picked = jnp.dot(pick, block, preferred_element_type=F32).astype(BF16)
        for s in range(slabs):
            lanes = slice(s * width, (s + 1) * width)
            at = (2 * chip + core) * slabs + s
            weights[at] = table[:, lanes]
            field[at + 1, 0:rows] = block[:, lanes]
            field[at + 1, rows:] = picked[:, lanes]


def split(ref, start, rows):
    return [ref.at[start + rows : start + rows + KROWS], ref.at[start : start + rows]]


def around(field, weights, spots):
    return [(field.at[s], field.at[s + 1], field.at[s + 2], weights.at[s]) for s in spots]


def inside(chip, weights):
    slabs = weights.shape[0] // 4
    return [chip * slabs + s for s in range(1, slabs - 1)]


def seam(chip, weights):
    middle = (2 * lax.div(chip, 2) + 1) * (weights.shape[0] // 4)
    return [middle - 1, middle]


def chip_kernel(sizes, mask, at, border, *refs):
    rows, terms, own, planes = sizes
    if mask:
        mine, table, other, *refs = refs
        _, _, total_in, squares_in, *refs = refs
        pieces = [[table, mine], split(other, at, rows)]
    else:
        mine, table, other, other_table, *refs = refs
        pieces = [[table, mine], [other_table, other]]
        total_in = None
    field, weights, total, squares, sides, right, left = refs
    j, _ = place()
    chip = jnp.bitwise_xor(lax.div(j, 2), mask)
    squares[...] = squares_in[...] if mask else jnp.zeros_like(squares)
    spread(chip, pieces, selector(own, rows, planes), field, weights, rows)
    spots = inside(chip, weights) + (seam(chip, weights) if border else [])
    act(around(field, weights, spots), across(field.shape[2]), sides, right, left, squares, rows, terms)
    depth = len(spots) * field.shape[2]
    contract(left, right, planes * own, terms, depth, total_in, keep(total))


def edge_kernel(*refs):
    pieces, strip = refs[:-1], refs[-1]
    j, _ = place()
    lines, cells = strip.shape
    parts = pieces[0].shape[0] // lines
    width = cells // parts
    for piece, flips in zip(pieces, (0, CORE, X, Y)):
        for here, lanes in ((0, slice(0, width)), (GROUP - 1, slice(cells - width, cells))):

            @pl.when(jnp.bitwise_xor(j, flips) == here)
            def _():
                for n in range(parts):
                    strip[:, n * width : (n + 1) * width] = piece[
                        n * lines : (n + 1) * lines, lanes
                    ]


def last_kernel(sizes, *refs):
    rows, terms, own, planes = sizes
    (one, two, strip, others_in, _, _, total_in, squares_in,
     field, weights, mine, others, levels, squares, sides, right, left) = refs
    slots, every, width = field.shape
    slabs = slots - 2
    lines = every - rows
    j, _ = place()
    chip = jnp.bitwise_xor(lax.div(j, 2), 3)
    pick = selector(own, rows, planes)
    squares[...] = squares_in[...]
    height = one.shape[0] + two.shape[0]
    even = jnp.bitwise_and(j, CORE) == 0
    size = strip.shape[0]
    other = others_in[height:, :]
    first_core = jnp.where(even, strip[...], other)
    second_core = jnp.where(even, other, strip[...])
    for at, source in ((0, second_core), (slots - 1, first_core)):
        for n in range(rows // size):
            field[at, n * size : (n + 1) * size] = source[:, n * width : (n + 1) * width]
        field[at, rows:] = jnp.dot(pick, field[at, 0:rows], preferred_element_type=F32).astype(BF16)
    part = one.shape[0] - KROWS
    there = others_in.at
    pieces = [
        [one.at[part:], one.at[0:part], two],
        [there[part : part + KROWS], there[0:part], there[part + KROWS : height]],
    ]
    spread(chip, pieces, pick, field, weights, rows)
    spots = inside(chip, weights) + seam(chip, weights)
    spots += [0, slabs // 2 - 1, slabs // 2, slabs - 1]
    act(around(field, weights, spots), across(width), sides, right, left, squares, rows, terms)
    lane = lax.broadcasted_iota(jnp.int32, (8, rows), 1)
    spare = jnp.zeros((8, rows), F32)
    powers = []
    for q in range(terms):
        level = jnp.sum(squares[q], keepdims=True)
        levels[q : q + 1, :] = jnp.broadcast_to(level, (1, levels.shape[1]))
        power = jnp.ceil(jnp.log2(jnp.maximum(level, 1e-30)))
        powers.append(power)
        level = level * jnp.exp2(-power)
        high = jnp.floor(level * 2.0**10) * 2.0**-10
        low = (level - high) * 2.0**10
        low = jnp.floor(low * 2.0**10) * 2.0**-10
        for n, value in enumerate((power, high, low)):
            spare = jnp.where(lane == 3 * q + n, value, spare)
    levels[terms:, :] = jnp.zeros((levels.shape[0] - terms, levels.shape[1]), F32)
    end = terms * (terms + 1) // 2 * own
    for z in range(1, planes):
        others[z - 1, end:, :] = spare[0 : others.shape[1] - end]

    def store(_, k, product):
        for q in range(k + 1):
            pair = q * terms - q * (q - 1) // 2 + k - q
            here = slice(pair * own, (pair + 1) * own)
            scale = jnp.exp2(TOP - jnp.ceil(0.5 * (powers[q] + powers[k])))
            for z in range(planes):
                block = product[q * lines + z * own : q * lines + (z + 1) * own, :]
                if z == 0:
                    mine[here, :] = block
                else:
                    others[z - 1, here, :] = block * scale

    contract(left, right, lines, terms, len(spots) * width, total_in, store)


def finish_kernel(own, terms, cells, *refs):
    parts, (levels, out) = refs[:-2], refs[-2:]
    rows = parts[0].shape[1]
    pairs = terms * (terms + 1) // 2
    spares = [part[pairs * own : pairs * own + 1, 0:128] for part in parts[1:]]
    norms = []
    powers = []
    for q in range(terms):
        level = levels[q : q + 1, 0:1]
        powers.append([])
        for spare in spares:
            power, high, low = (spare[:, 3 * q + n : 3 * q + n + 1] for n in range(3))
            level = level + (high + low * 2.0**-10) * jnp.exp2(power)
            powers[q].append(power)
        norms.append(lax.rsqrt(level / (rows * cells) + 1e-06) * cells**-0.5)
    pair = 0
    for q in range(terms):
        for k in range(q, terms):
            here = slice(pair * own, (pair + 1) * own)
            total = parts[0][here, :]
            for n, part in enumerate(parts[1:]):
                power = jnp.ceil(0.5 * (powers[q][n] + powers[k][n])) - TOP
                total = total + part[here, :] * jnp.exp2(power)
            out[:, pair, :] = total * (norms[q] * norms[k])
            pair += 1


def per_device(basis, slab_region, coef_index, coef_table):
    terms = coef_index.shape[1]
    rows, cells = basis.shape
    width = cells // slab_region.shape[0]
    count = lax.axis_size("mode")
    planes = count // GROUP
    own = rows // count
    lines = planes * own
    every = rows + lines
    pairs = terms * (terms + 1) // 2
    slabs = 2 * slab_region.shape[0]
    sizes = (rows, terms, own, planes)

    plane = (
        shape((GROUP // 2 * slabs + 2, every, width), BF16),
        shape((GROUP // 2 * slabs, KROWS, width), BF16),
    )
    sums = (shape((pairs * lines, rows)), shape((terms, 8, width)))

    def scratch(number):
        return [
            pltpu.VMEM((2, every, 2 * width), F32),
            pltpu.VMEM((terms, rows, number * width), BF16),
            pltpu.VMEM((terms * lines, number * width), BF16),
        ]

    def chip(mask, at, border):
        return call(
            functools.partial(chip_kernel, sizes, mask, at, border),
            plane + sums,
            scratch(slabs if border else slabs - 2),
            aliases={3: 0, 4: 1} if mask else None,
        )

    by_x = flip(basis, X, count)
    by_y = flip(basis, Y, count)
    by_core = flip(basis, CORE, count)
    by_core, slab_region = lax.optimization_barrier((by_core, slab_region))
    table = weight_rows(cells, slab_region, coef_index, coef_table)
    table_core = flip(table, CORE, count)
    table_x = flip(table, X, count)
    table_y = flip(table, Y, count)
    field, weights, total, squares = chip(0, 0, False)(basis, table, by_core, table_core)
    by_x, by_y, table_x, table_y, total = lax.optimization_barrier(
        (by_x, by_y, table_x, table_y, total)
    )

    half = (rows - KROWS) // 2
    one = flip(jnp.concatenate([by_x[:half], table_x], axis=0), Y, count)
    two = flip(by_y[half:], X, count)
    others = flip(jnp.concatenate([by_x, table_x, by_y, table_y], axis=0), CORE, count)
    strip = call(edge_kernel, shape((rows * width // cells, cells), BF16))(
        basis, by_core, by_x, by_y
    )
    pairs_of = []
    for i in range(count):
        here = i % GROUP
        if here in (0, 1, 2, 4):
            to = (i - here - GROUP) % count + (6 if here == 1 else here)
        else:
            to = (i - here + GROUP) % count + (1 if here == 6 else here)
        pairs_of.append((i, to))
    strip = lax.ppermute(strip, "mode", pairs_of)
    field, weights, total, squares = chip(1, 0, True)(
        by_x, table_x, others, field, weights, total, squares
    )
    one, two, strip, total = lax.optimization_barrier((one, two, strip, total))

    diagonal = flip(jnp.concatenate([one, two, strip], axis=0), CORE, count)
    field, weights, total, squares = chip(2, rows + KROWS, False)(
        by_y, table_y, others, field, weights, total, squares
    )
    diagonal, total = lax.optimization_barrier((diagonal, total))

    height = pairs * own + 8 - (pairs * own) % 8
    _, _, mine, others, levels = call(
        functools.partial(last_kernel, sizes),
        plane + (shape((height, rows)), shape((planes - 1, height, rows)), shape((8, 128))),
        [pltpu.VMEM(sums[1].shape, F32)] + scratch(slabs + 4),
        aliases={4: 0, 5: 1},
    )(one, two, strip, diagonal, field, weights, total, squares)

    parts = [mine]
    others = others.astype(jnp.float16)
    for z in range(1, planes):
        there = [(i, (i + z * GROUP) % count) for i in range(count)]
        parts.append(lax.ppermute(others[z - 1], "mode", there).astype(F32))
    out = call(
        functools.partial(finish_kernel, own, terms, cells * count), shape((own, pairs, rows))
    )(*parts, levels)
    return jnp.transpose(out, (1, 0, 2))


def solution(mesh):
    return jax.shard_map(
        per_device,
        mesh=mesh,
        in_specs=(P("groups", "mode"), P(("groups", "mode")), P("groups", None), P("groups")),
        out_specs=P(None, ("groups", "mode"), None),
        check_vma=False,
    )
```

```python
import functools

import jax
import jax.numpy as jnp
from jax import lax
from jax.experimental import pallas as pl
from jax.experimental.pallas import tpu as pltpu
from jax.sharding import PartitionSpec as P

GROUP = 8
CORE, X, Y = 1, 2, 4
KROWS = 32
TOP = 14.0
F32 = jnp.float32
BF16 = jnp.bfloat16
VMEM = pl.BlockSpec(memory_space=pltpu.VMEM)
HBM = pl.BlockSpec(memory_space=pltpu.HBM)


def call(kernel, outs, scratch=(), aliases=None, ins=None):
    def run(*args):
        return pl.pallas_call(
            kernel,
            out_shape=outs,
            in_specs=[VMEM] * len(args) if ins is None else ins,
            out_specs=jax.tree.map(lambda _: VMEM, outs),
            scratch_shapes=list(scratch),
            input_output_aliases=aliases or {},
            compiler_params=pltpu.CompilerParams(vmem_limit_bytes=32 * 1024 * 1024),
            cost_estimate=pl.CostEstimate(flops=0, bytes_accessed=0, transcendentals=0),
        )(*args)

    return run


def shape(dims, dtype=F32):
    return jax.ShapeDtypeStruct(dims, dtype)


def place():
    me = lax.axis_index("mode")
    return lax.rem(me, GROUP), lax.div(me, GROUP)


def steps(planes):
    if planes & (planes - 1):
        return list(range(1, planes))
    order = []
    while planes > 1:
        order += range(planes // 2, planes)
        planes //= 2
    return order


def partner(a, k, planes):
    step = ([0] + steps(planes))[k]
    return (a + step) % planes if planes & (planes - 1) else a ^ step


def flip(values, mask, count):
    return lax.ppermute(values, "mode", [(i, i ^ mask) for i in range(count)])


def weight_kernel(region, index, table, out, region_s, index_s, table_s, sems):
    copies = [
        pltpu.make_async_copy(region, region_s, sems.at[0]),
        pltpu.make_async_copy(index, index_s, sems.at[1]),
        pltpu.make_async_copy(table, table_s, sems.at[2]),
    ]
    for copy in copies:
        copy.start()
    for copy in copies:
        copy.wait()
    slabs = region.shape[0]
    width = out.shape[1] // slabs
    terms = index.shape[0]
    entries = table.shape[0]
    row = lax.broadcasted_iota(jnp.int32, (KROWS, width), 0)
    for s in range(slabs):
        reg = region_s[s]
        block = jnp.zeros((KROWS, width), F32)
        for q in range(terms):
            at = index_s[q, reg]
            kappa = jnp.where(at < entries, table_s[jnp.minimum(at, entries - 1)], 0.0)
            block = jnp.where(lax.div(row, 3) == q, kappa, block)
        high = block.astype(BF16).astype(F32)
        mid = (block - high).astype(BF16).astype(F32)
        low = block - high - mid
        part = lax.rem(row, 3)
        block = jnp.where(part == 0, high, jnp.where(part == 1, mid, low))
        out[:, s * width : (s + 1) * width] = block.astype(BF16)


def weight_rows(cells, region, index, table):
    return call(
        weight_kernel,
        shape((KROWS, cells), BF16),
        [
            pltpu.SMEM(region.shape, jnp.int32),
            pltpu.SMEM(index.shape[::-1], jnp.int32),
            pltpu.SMEM(table.shape, F32),
            pltpu.SemaphoreType.DMA((3,)),
        ],
        ins=[HBM] * 3,
    )(region, index.T, table)


def selector(own, rows, planes):
    j, a = place()
    line = lax.broadcasted_iota(jnp.int32, (planes * own, rows), 0)
    column = lax.broadcasted_iota(jnp.int32, (planes * own, rows), 1)
    shift = jnp.zeros((planes * own, rows), jnp.int32)
    for k in range(planes):
        start = partner(a, k, planes) * (GROUP * own) + j * own - k * own
        shift = jnp.where(line >= k * own, start, shift)
    return jnp.where(column - line == shift, 1.0, 0.0).astype(BF16)


def across(width):
    line = lax.broadcasted_iota(jnp.int32, (width, width), 0)
    column = lax.broadcasted_iota(jnp.int32, (width, width), 1)
    same = jnp.where(line == column, 1.0, 0.0)
    beside = jnp.where(jnp.abs(line - column) == 1, 1.0, 0.0)
    mirror = jnp.where(line + column == width - 1, 1.0, 0.0)
    return jnp.concatenate([2.0 * same - beside, same - mirror], axis=1).astype(BF16)


def act(triples, stencil, sides, right, left, squares, rows, terms):
    total, width = triples[0][1].shape
    own = total - rows
    for n, (before, here, after, weight) in enumerate(triples):
        lanes = slice(n * width, (n + 1) * width)
        side = sides.at[n % 2]
        side[...] = jnp.dot(here[...], stencil, preferred_element_type=F32)
        table = weight[...].astype(F32)
        kappas = []
        for q in range(terms):
            one = (table[3 * q : 3 * q + 1] + table[3 * q + 1 : 3 * q + 2]) + table[
                3 * q + 2 : 3 * q + 3
            ]
            kappas.append(jnp.broadcast_to(one, (8, width))[None])
        sums = [jnp.zeros((8, width), F32) for _ in range(terms)]
        for start in range(0, total, own):
            part = slice(start, start + own)
            value = here[part, :].astype(F32)
            back = value - before[part, :].astype(F32)
            ahead = value - after[part, :].astype(F32)
            shapes = (
                back + ahead,
                side[part, 0:width],
                back,
                ahead,
                side[part, width : 2 * width],
                value,
            )
            for q in range(terms):
                action = shapes[q].reshape(own // 8, 8, width) * kappas[q]
                action = action.reshape(own, width).astype(BF16)
                if start < rows:
                    right[q, part, lanes] = action
                    rounded = action.astype(F32).reshape(own // 8, 8, width)
                    sums[q] += jnp.sum(rounded * rounded, axis=0)
                else:
                    left[q * own : (q + 1) * own, lanes] = action
        for q in range(terms):
            squares[q] += sums[q]


def contract(left, right, own, terms, depth, before, store):
    offset = 0
    for k in range(terms):
        lines = own * (k + 1)
        product = lax.dot_general(
            left[0:lines, 0:depth],
            right[k, :, 0:depth],
            (((1,), (1,)), ((), ())),
            preferred_element_type=F32,
        )
        if before is not None:
            product = before[offset : offset + lines, :] + product
        store(offset, k, product)
        offset += lines


def keep(total):
    def store(offset, _, product):
        total[offset : offset + product.shape[0], :] = product

    return store


def spread(chip, pieces, pick, field, weights, rows):
    j, _ = place()
    width = field.shape[2]
    for flipped, (table, *parts) in enumerate(pieces):
        core = jnp.bitwise_xor(jnp.bitwise_and(j, 1), flipped)
        slabs = table.shape[1] // width
        block = jnp.concatenate([part[...] for part in parts], axis=0)
        picked = jnp.dot(pick, block, preferred_element_type=F32).astype(BF16)
        for s in range(slabs):
            lanes = slice(s * width, (s + 1) * width)
            at = (2 * chip + core) * slabs + s
            weights[at] = table[:, lanes]
            field[at + 1, 0:rows] = block[:, lanes]
            field[at + 1, rows:] = picked[:, lanes]


def split(ref, start, rows):
    return [ref.at[start + rows : start + rows + KROWS], ref.at[start : start + rows]]


def around(field, weights, spots):
    return [(field.at[s], field.at[s + 1], field.at[s + 2], weights.at[s]) for s in spots]


def inside(chip, weights):
    slabs = weights.shape[0] // 4
    return [chip * slabs + s for s in range(1, slabs - 1)]


def seam(chip, weights):
    middle = (2 * lax.div(chip, 2) + 1) * (weights.shape[0] // 4)
    return [middle - 1, middle]


def chip_kernel(sizes, mask, at, border, *refs):
    rows, terms, own, planes = sizes
    if mask:
        mine, table, other, *refs = refs
        _, _, total_in, squares_in, *refs = refs
        pieces = [[table, mine], split(other, at, rows)]
    else:
        mine, table, other, other_table, *refs = refs
        pieces = [[table, mine], [other_table, other]]
        total_in = None
    field, weights, total, squares, sides, right, left = refs
    j, _ = place()
    chip = jnp.bitwise_xor(lax.div(j, 2), mask)
    squares[...] = squares_in[...] if mask else jnp.zeros_like(squares)
    spread(chip, pieces, selector(own, rows, planes), field, weights, rows)
    spots = inside(chip, weights) + (seam(chip, weights) if border else [])
    act(around(field, weights, spots), across(field.shape[2]), sides, right, left, squares, rows, terms)
    depth = len(spots) * field.shape[2]
    contract(left, right, planes * own, terms, depth, total_in, keep(total))


def edge_kernel(*refs):
    pieces, strip = refs[:-1], refs[-1]
    j, _ = place()
    lines, cells = strip.shape
    parts = pieces[0].shape[0] // lines
    width = cells // parts
    for piece, flips in zip(pieces, (0, CORE, X, Y)):
        for here, lanes in ((0, slice(0, width)), (GROUP - 1, slice(cells - width, cells))):

            @pl.when(jnp.bitwise_xor(j, flips) == here)
            def _():
                for n in range(parts):
                    strip[:, n * width : (n + 1) * width] = piece[
                        n * lines : (n + 1) * lines, lanes
                    ]


def last_kernel(sizes, *refs):
    rows, terms, own, planes = sizes
    (one, two, strip, others_in, _, _, total_in, squares_in,
     field, weights, mine, others, levels, squares, sides, right, left) = refs
    slots, every, width = field.shape
    slabs = slots - 2
    lines = every - rows
    j, _ = place()
    chip = jnp.bitwise_xor(lax.div(j, 2), 3)
    pick = selector(own, rows, planes)
    squares[...] = squares_in[...]
    height = one.shape[0] + two.shape[0]
    even = jnp.bitwise_and(j, CORE) == 0
    size = strip.shape[0]
    other = others_in[height:, :]
    first_core = jnp.where(even, strip[...], other)
    second_core = jnp.where(even, other, strip[...])
    for at, source in ((0, second_core), (slots - 1, first_core)):
        for n in range(rows // size):
            field[at, n * size : (n + 1) * size] = source[:, n * width : (n + 1) * width]
        field[at, rows:] = jnp.dot(pick, field[at, 0:rows], preferred_element_type=F32).astype(BF16)
    part = one.shape[0] - KROWS
    there = others_in.at
    pieces = [
        [one.at[part:], one.at[0:part], two],
        [there[part : part + KROWS], there[0:part], there[part + KROWS : height]],
    ]
    spread(chip, pieces, pick, field, weights, rows)
    spots = inside(chip, weights) + seam(chip, weights)
    spots += [0, slabs // 2 - 1, slabs // 2, slabs - 1]
    act(around(field, weights, spots), across(width), sides, right, left, squares, rows, terms)
    lane = lax.broadcasted_iota(jnp.int32, (8, rows), 1)
    spare = jnp.zeros((8, rows), F32)
    powers = []
    for q in range(terms):
        level = jnp.sum(squares[q], keepdims=True)
        levels[q : q + 1, :] = jnp.broadcast_to(level, (1, levels.shape[1]))
        power = jnp.ceil(jnp.log2(jnp.maximum(level, 1e-30)))
        powers.append(power)
        level = level * jnp.exp2(-power)
        high = jnp.floor(level * 2.0**10) * 2.0**-10
        low = (level - high) * 2.0**10
        low = jnp.floor(low * 2.0**10) * 2.0**-10
        for n, value in enumerate((power, high, low)):
            spare = jnp.where(lane == 3 * q + n, value, spare)
    levels[terms:, :] = jnp.zeros((levels.shape[0] - terms, levels.shape[1]), F32)
    end = terms * (terms + 1) // 2 * own
    for z in range(1, planes):
        others[z - 1, end:, :] = spare[0 : others.shape[1] - end]

    def store(_, k, product):
        for q in range(k + 1):
            pair = q * terms - q * (q - 1) // 2 + k - q
            here = slice(pair * own, (pair + 1) * own)
            scale = jnp.exp2(TOP - jnp.ceil(0.5 * (powers[q] + powers[k])))
            for z in range(planes):
                block = product[q * lines + z * own : q * lines + (z + 1) * own, :]
                if z == 0:
                    mine[here, :] = block
                else:
                    others[z - 1, here, :] = block * scale

    contract(left, right, lines, terms, len(spots) * width, total_in, store)


def finish_kernel(own, terms, cells, *refs):
    parts, (levels, out) = refs[:-2], refs[-2:]
    rows = parts[0].shape[1]
    pairs = terms * (terms + 1) // 2
    spares = [part[pairs * own : pairs * own + 1, 0:128] for part in parts[1:]]
    norms = []
    powers = []
    for q in range(terms):
        level = levels[q : q + 1, 0:1]
        powers.append([])
        for spare in spares:
            power, high, low = (spare[:, 3 * q + n : 3 * q + n + 1] for n in range(3))
            level = level + (high + low * 2.0**-10) * jnp.exp2(power)
            powers[q].append(power)
        norms.append(lax.rsqrt(level / (rows * cells) + 1e-06) * cells**-0.5)
    pair = 0
    for q in range(terms):
        for k in range(q, terms):
            here = slice(pair * own, (pair + 1) * own)
            total = parts[0][here, :]
            for n, part in enumerate(parts[1:]):
                power = jnp.ceil(0.5 * (powers[q][n] + powers[k][n])) - TOP
                total = total + part[here, :] * jnp.exp2(power)
            out[:, pair, :] = total * (norms[q] * norms[k])
            pair += 1


def per_device(basis, slab_region, coef_index, coef_table):
    terms = coef_index.shape[1]
    rows, cells = basis.shape
    width = cells // slab_region.shape[0]
    count = lax.axis_size("mode")
    planes = count // GROUP
    own = rows // count
    lines = planes * own
    every = rows + lines
    pairs = terms * (terms + 1) // 2
    slabs = 2 * slab_region.shape[0]
    sizes = (rows, terms, own, planes)

    plane = (
        shape((GROUP // 2 * slabs + 2, every, width), BF16),
        shape((GROUP // 2 * slabs, KROWS, width), BF16),
    )
    sums = (shape((pairs * lines, rows)), shape((terms, 8, width)))

    def scratch(number):
        return [
            pltpu.VMEM((2, every, 2 * width), F32),
            pltpu.VMEM((terms, rows, number * width), BF16),
            pltpu.VMEM((terms * lines, number * width), BF16),
        ]

    def chip(mask, at, border):
        return call(
            functools.partial(chip_kernel, sizes, mask, at, border),
            plane + sums,
            scratch(slabs if border else slabs - 2),
            aliases={3: 0, 4: 1} if mask else None,
        )

    by_x = flip(basis, X, count)
    by_y = flip(basis, Y, count)
    by_core = flip(basis, CORE, count)
    by_core, slab_region = lax.optimization_barrier((by_core, slab_region))
    table = weight_rows(cells, slab_region, coef_index, coef_table)
    table_core = flip(table, CORE, count)
    table_x = flip(table, X, count)
    table_y = flip(table, Y, count)
    field, weights, total, squares = chip(0, 0, False)(basis, table, by_core, table_core)
    by_x, by_y, total = lax.optimization_barrier((by_x, by_y, total))

    half = (rows - KROWS) // 2
    one = flip(jnp.concatenate([by_x[:half], table_x], axis=0), Y, count)
    two = flip(by_y[half:], X, count)
    others = flip(jnp.concatenate([by_x, table_x, by_y, table_y], axis=0), CORE, count)
    strip = call(edge_kernel, shape((rows * width // cells, cells), BF16))(
        basis, by_core, by_x, by_y
    )
    pairs_of = []
    for i in range(count):
        here = i % GROUP
        if here in (0, 1, 2, 4):
            to = (i - here - GROUP) % count + (6 if here == 1 else here)
        else:
            to = (i - here + GROUP) % count + (1 if here == 6 else here)
        pairs_of.append((i, to))
    strip = lax.ppermute(strip, "mode", pairs_of)
    field, weights, total, squares = chip(1, 0, True)(
        by_x, table_x, others, field, weights, total, squares
    )
    one, two, strip, total = lax.optimization_barrier((one, two, strip, total))

    diagonal = flip(jnp.concatenate([one, two, strip], axis=0), CORE, count)
    field, weights, total, squares = chip(2, rows + KROWS, False)(
        by_y, table_y, others, field, weights, total, squares
    )
    diagonal, total = lax.optimization_barrier((diagonal, total))

    height = pairs * own + 8 - (pairs * own) % 8
    _, _, mine, others, levels = call(
        functools.partial(last_kernel, sizes),
        plane + (shape((height, rows)), shape((planes - 1, height, rows)), shape((8, 128))),
        [pltpu.VMEM(sums[1].shape, F32)] + scratch(slabs + 4),
        aliases={4: 0, 5: 1},
    )(one, two, strip, diagonal, field, weights, total, squares)

    parts = [mine]
    others = others.astype(jnp.float16)
    for z in range(1, planes):
        there = [(i, partner(i // GROUP, z, planes) * GROUP + i % GROUP) for i in range(count)]
        parts.append(lax.ppermute(others[z - 1], "mode", there).astype(F32))
    out = call(
        functools.partial(finish_kernel, own, terms, cells * count), shape((own, pairs, rows))
    )(*parts, levels)
    return jnp.transpose(out, (1, 0, 2))


def solution(mesh):
    return jax.shard_map(
        per_device,
        mesh=mesh,
        in_specs=(P("groups", "mode"), P(("groups", "mode")), P("groups", None), P("groups")),
        out_specs=P(None, ("groups", "mode"), None),
        check_vma=False,
    )
```
